32 devices in a mesh: ctx: 8 (over z, x), tp: 4 (over y, core).
Axes of the slice: x: 2, y: 2, z: 4, core: 2. Of those that a mesh axis runs over, the one named last changes fastest.
Arguments:
- x_raw: bfloat16 [1024, 4096], P('ctx', 'tp'), may hold values from -6 to 6
- b_raw: bfloat16 [1024, 512], P('ctx'), may hold values from -0.59765625 to 0.59765625
- c_raw: bfloat16 [1024, 512], P('ctx'), may hold values from -0.59765625 to 0.59765625
- z_gate: bfloat16 [1024, 4096], P('ctx', 'tp'), may hold values from -6 to 6
- dt_raw: float32 [1024, 128], P('ctx', 'tp'), may hold values from -4 to 4
- conv_x: float32 [4, 4096], P(None, 'tp'), may hold values from -3 to 3
- conv_b: float32 [4, 512], replicated, may hold values from -3 to 3
- conv_c: float32 [4, 512], replicated, may hold values from -3 to 3
- dt_bias: float32 [128], P('tp'), may hold values from -1 to 1
- a_log: float32 [128], P('tp'), may hold values from -14 to -3
- d_skip: float32 [128], P('tp'), may hold values from 0.5 to 1.5
- gain: float32 [4096], P('tp'), may hold values from 0.5 to 1.5
- grad_out: bfloat16 [1024, 4096], P('ctx', 'tp'), may hold values from -6 to 6
Outputs:
- grad_x_raw: bfloat16 [1024, 4096], P('ctx', 'tp')
- grad_b_raw: bfloat16 [1024, 512], P('ctx')
- grad_c_raw: bfloat16 [1024, 512], P('ctx')
- grad_z_gate: bfloat16 [1024, 4096], P('ctx', 'tp')
- grad_dt_raw: float32 [1024, 128], P('ctx', 'tp')
- grad_conv_x: float32 [4, 4096], P(None, 'tp')
- grad_conv_b: float32 [4, 512], replicated
- grad_conv_c: float32 [4, 512], replicated
- grad_dt_bias: float32 [128], P('tp')
- grad_a_log: float32 [128], P('tp')
- grad_d_skip: float32 [128], P('tp')
- grad_gain: float32 [4096], P('tp')
The draws below stay inside these ranges and needn't reach their ends.
All inputs are finite; a program needn't handle non-finite values.
Results may differ from the reference program's by a relative error of at most 0.00105.
Values may be sent and summed in bfloat16 or wider, within the bound.
A program may use at most 192 MiB of HBM per device.

```python
import jax
import jax.numpy as jnp
from jax import lax

HEADS = 128
HEAD_DIM = 32
STATE = 128
GROUPS = 4
CONV = 4
SPAN = 128
TOKENS = 1024


def draw_a_log(key, part):
    pick_key, level_key = jax.random.split(jax.random.fold_in(key, 11))
    levels = jax.random.uniform(level_key, (HEADS,), jnp.float32)
    slow_share = 0.5
    slow_value = jnp.log(0.15 / TOKENS) + levels * jnp.log(10.0)
    fast_value = jnp.log(1.0 / 60.0) + levels * jnp.log(2.4)
    slow_pick = jax.random.uniform(pick_key, (HEADS,), jnp.float32) < slow_share
    return jnp.where(slow_pick, slow_value, fast_value).astype(jnp.float32)


def block_scale(own_key, dims, cuts, least, top_value):
    level = 1.0
    for position, blocks in cuts:
        heights = jax.random.uniform(jax.random.fold_in(jax.random.fold_in(own_key, 6), position), (blocks,), jnp.float32, least / len(cuts), top_value / len(cuts))
        level = level * jnp.repeat(jnp.exp(heights), dims[position] // blocks).reshape((-1,) + (1,) * (len(dims) - 1 - position))
    return level


def noise(key, dims, deviation, most, shards=(), kind=jnp.bfloat16):
    entries = deviation * jax.random.normal(key, dims, jnp.float32)
    if shards:
        entries = entries * block_scale(key, dims, shards, -0.22, 0.18)
    return jnp.clip(entries, -most, most).astype(kind)


def setup_inputs(seed: int = 0) -> dict:
    seeds = jax.random.split(jax.random.key(seed), 14)
    x_raw = noise(seeds[0], (TOKENS, HEADS * HEAD_DIM), 1.0, 6.0, ((0, 8), (1, 4)))
    b_raw = noise(seeds[1], (TOKENS, GROUPS * STATE), 0.1, 0.59765625, ((0, 8),))
    c_raw = noise(seeds[2], (TOKENS, GROUPS * STATE), 0.1, 0.59765625, ((0, 8),))
    z_gate = noise(seeds[3], (TOKENS, HEADS * HEAD_DIM), 1.0, 6.0, ((0, 8), (1, 4)))
    dt_raw = noise(seeds[4], (TOKENS, HEADS), 1.0, 4.0, ((0, 8), (1, 4)), jnp.float32)
    conv_x = noise(seeds[5], (CONV, HEADS * HEAD_DIM), CONV ** -0.5, 3.0, ((1, 4),), jnp.float32)
    conv_b = noise(seeds[6], (CONV, GROUPS * STATE), CONV ** -0.5, 3.0, (), jnp.float32)
    conv_c = noise(seeds[7], (CONV, GROUPS * STATE), CONV ** -0.5, 3.0, (), jnp.float32)
    dt_bias = jnp.clip(jax.random.uniform(seeds[8], (HEADS,), jnp.float32, -1.0, 1.0) * block_scale(seeds[8], (HEADS,), ((0, 4),), -0.4, 0.0), -1.0, 1.0)
    a_log = draw_a_log(jax.random.fold_in(seeds[13], 71), 0)
    d_skip = jnp.clip(0.5 + 1.0 * jax.random.uniform(seeds[10], (HEADS,), jnp.float32) ** block_scale(seeds[10], (HEADS,), ((0, 4),), -0.2, 0.2), 0.5, 1.5)
    gain = jnp.clip(0.5 + 1.0 * jax.random.uniform(seeds[11], (HEADS * HEAD_DIM,), jnp.float32) ** block_scale(seeds[11], (HEADS * HEAD_DIM,), ((0, 4),), -0.2, 0.2), 0.5, 1.5)
    grad_out = noise(seeds[12], (TOKENS, HEADS * HEAD_DIM), 1.0, 6.0, ((0, 8), (1, 4)))
    return {"x_raw": x_raw, "b_raw": b_raw, "c_raw": c_raw, "z_gate": z_gate, "dt_raw": dt_raw, "conv_x": conv_x, "conv_b": conv_b, "conv_c": conv_c, "dt_bias": dt_bias, "a_log": a_log, "d_skip": d_skip, "gain": gain, "grad_out": grad_out}


PRECISE = lax.Precision.HIGHEST
EPSILON = 1e-05

def shifted_conv(extended, weight):
    tap_count = weight.shape[0]
    length = extended.shape[0] - tap_count + 1
    total = weight[0] * extended[0:length]
    for offset in range(1, tap_count):
        total = total + weight[offset] * extended[offset:offset + length]
    return jax.nn.silu(total)

def causal_conv(raw_rows, weight):
    padding = jnp.zeros((weight.shape[0] - 1, raw_rows.shape[1]), raw_rows.dtype)
    return shifted_conv(jnp.concatenate([padding, raw_rows], axis=0), weight)

def span_output(x_blk, b_blk, c_blk, dt_blk, cum_decay, skip_gain, states):
    length = x_blk.shape[1]
    causal = jnp.arange(length)[:, None] >= jnp.arange(length)[None, :]
    pair_inner = jnp.einsum('cqgn,csgn->cgqs', c_blk, b_blk, precision=PRECISE)
    cum_cols = jnp.transpose(cum_decay, (0, 2, 3, 1))
    spread = cum_cols[..., :, None] - cum_cols[..., None, :]
    weights = jnp.where(causal, jnp.exp(jnp.where(causal, spread, 0.0)), 0.0)
    dt_cols = jnp.transpose(dt_blk, (0, 2, 3, 1))
    weights = weights * pair_inner[:, None] * dt_cols[..., None, :]
    diagonal = jnp.einsum('crgqs,csrgp->cqrgp', weights, x_blk, precision=PRECISE)
    carried = jnp.einsum('cqgn,crgpn->cqrgp', c_blk, states, precision=PRECISE)
    carried = carried * jnp.exp(cum_decay)[..., None]
    return diagonal + carried + skip_gain[:, :, None] * x_blk

def span_state(x_blk, b_blk, dt_blk, cum_decay):
    weight_rows = jnp.exp(cum_decay[:, -1:] - cum_decay) * dt_blk
    weighted = weight_rows[..., None] * x_blk
    return jnp.einsum('cqrgp,cqgn->crgpn', weighted, b_blk, precision=PRECISE)

def forward(x_raw, b_raw, c_raw, z_gate, dt_raw, conv_x, conv_b, conv_c, dt_bias, a_log, d_skip, gain):
    length = x_raw.shape[0]
    per_group = HEADS // GROUPS
    blocks = length // SPAN
    x_act = causal_conv(x_raw, conv_x).reshape(blocks, SPAN, per_group, GROUPS, HEAD_DIM)
    b_act = causal_conv(b_raw, conv_b).reshape(blocks, SPAN, GROUPS, STATE)
    c_act = causal_conv(c_raw, conv_c).reshape(blocks, SPAN, GROUPS, STATE)
    step_dt = jax.nn.softplus(dt_raw + dt_bias).reshape(blocks, SPAN, per_group, GROUPS)
    decay_rate = jnp.exp(a_log).reshape(per_group, GROUPS)
    skip_gain = d_skip.reshape(per_group, GROUPS)

    def advance_plain(carry_state, pieces):
        x_blk = pieces[0][None]
        b_blk = pieces[1][None]
        c_blk = pieces[2][None]
        dt_blk = pieces[3][None]
        cum_decay = jnp.cumsum(-decay_rate * dt_blk, axis=1)
        output = span_output(x_blk, b_blk, c_blk, dt_blk, cum_decay, skip_gain, carry_state[None])
        own_state = span_state(x_blk, b_blk, dt_blk, cum_decay)[0]
        carry_state = jnp.exp(cum_decay[0, -1])[..., None, None] * carry_state + own_state
        return (carry_state, output[0])
    advance = jax.checkpoint(advance_plain)
    initial = jnp.zeros((per_group, GROUPS, HEAD_DIM, STATE), jnp.float32)
    finished, outputs = lax.scan(advance, initial, (x_act, b_act, c_act, step_dt))
    ssd_out = outputs.reshape(length, HEADS * HEAD_DIM)
    gated_out = ssd_out * jax.nn.silu(z_gate)
    grouped = gated_out.reshape(length, per_group, GROUPS, HEAD_DIM)
    mean_square = lax.optimization_barrier(jnp.mean(grouped * grouped, axis=(1, 3), keepdims=True))
    normed = (grouped * lax.rsqrt(mean_square + EPSILON)).reshape(length, HEADS * HEAD_DIM)
    return normed * gain

def reference(x_raw, b_raw, c_raw, z_gate, dt_raw, conv_x, conv_b, conv_c, dt_bias, a_log, d_skip, gain, grad_out):
    primals = (x_raw.astype(jnp.float32), b_raw.astype(jnp.float32), c_raw.astype(jnp.float32), z_gate.astype(jnp.float32), dt_raw, conv_x, conv_b, conv_c, dt_bias, a_log, d_skip, gain)
    normed, pullback = jax.vjp(forward, *primals)
    grads = pullback(grad_out.astype(jnp.float32))
    return (grads[0].astype(jnp.bfloat16), grads[1].astype(jnp.bfloat16), grads[2].astype(jnp.bfloat16), grads[3].astype(jnp.bfloat16), grads[4], grads[5], grads[6], grads[7], grads[8], grads[9], grads[10], grads[11])
```

```python
import functools

import jax
import jax.numpy as jnp
from jax import lax
from jax.experimental import pallas as pl
from jax.experimental.pallas import tpu as pltpu
from jax.sharding import PartitionSpec as P

HEAD_DIM = 32
STATE = 128
GROUPS = 4
CONV = 4
HALO = 16
LANES = 128
EPSILON = 1e-05
F32 = jnp.float32
BF16 = jnp.bfloat16
MM = ((1,), (0,))
MT = ((1,), (1,))


def split(value):
    high = value.astype(BF16)
    return high, (value - high.astype(F32)).astype(BF16)


def mul(a, b, dims=MM):
    def dot(u, v):
        return lax.dot_general(u, v, (dims, ((), ())), preferred_element_type=F32)

    return dot(a[0], b[0]) + (dot(a[0], b[1]) + dot(a[1], b[0]))


def exact(a, b, dims=MM):
    return lax.dot_general(
        a, b, (dims, ((), ())), preferred_element_type=F32, precision=lax.Precision.HIGHEST
    )


def sigmoid(v):
    return 1.0 / (1.0 + jnp.exp(-v))


def silu_slope(v):
    s = sigmoid(v)
    return s * (1.0 + v * (1.0 - s))


def iota(shape, axis):
    return lax.broadcasted_iota(jnp.int32, shape, axis)


def lane_group(width):
    return (iota((1, width), 1) // HEAD_DIM) % GROUPS


def head_spread(heads, width):
    return (iota((heads, width), 1) // HEAD_DIM == iota((heads, width), 0)).astype(F32)


def block_diagonal(state):
    owner = lane_group(state.shape[1])
    return jnp.concatenate([jnp.where(owner == g, state, 0.0) for g in range(GROUPS)], axis=0)


def diagonal_blocks(stacked):
    owner = lane_group(stacked.shape[1])
    total = jnp.zeros((STATE, stacked.shape[1]), F32)
    for g in range(GROUPS):
        total = jnp.where(owner == g, stacked[g * STATE : (g + 1) * STATE], total)
    return total


def tiles(width, size):
    return [slice(i, i + size) for i in range(0, width, size)]


def conv_rows(ext, taps, rows, cols):
    total = taps[0:1, :] * ext[HALO - 3 : HALO - 3 + rows, cols]
    for k in range(1, CONV):
        total = total + taps[k : k + 1, :] * ext[HALO - 3 + k : HALO - 3 + k + rows, cols]
    return total


def begin_kernel(
    x_ref, b_ref, c_ref, halo_ref, dt_ref, cx_ref, cb_ref, cc_ref, bias_ref, alog_ref,
    prex_ref, x_out, prebc_ref, bc_ref, dt_out, cum_ref, cumt_ref, dtx_ref, cumx_ref, state_ref, dec_ref,
    ext,
):
    rows, width = x_ref.shape
    half = b_ref.shape[1]
    heads = dt_ref.shape[1]
    step = jax.nn.softplus(dt_ref[...] + bias_ref[...])
    dt_out[...] = step
    tril = (iota((rows, rows), 0) >= iota((rows, rows), 1)).astype(F32)
    cum = exact(tril, -jnp.exp(alog_ref[...]) * step)
    cum_ref[...] = cum
    cumt_ref[...] = jnp.transpose(cum)
    spread = head_spread(heads, width)
    dtx_ref[...] = exact(step, spread)
    cumx_ref[...] = exact(cum, spread)
    dec_ref[...] = jnp.exp(cumx_ref[rows - 1 : rows, :])
    ext[0:HALO, :] = halo_ref[:, 0:width].astype(F32)
    ext[HALO:, :] = x_ref[...].astype(F32)
    for cols in tiles(width, LANES):
        pre = conv_rows(ext, cx_ref[:, cols], rows, cols)
        prex_ref[:, cols] = pre
        x_out[:, cols] = pre * sigmoid(pre)
    ext[0:HALO, :] = halo_ref[:, width:].astype(F32)
    ext[HALO:, 0:half] = b_ref[...].astype(F32)
    ext[HALO:, half:] = c_ref[...].astype(F32)
    for cols in tiles(2 * half, LANES):
        taps = cb_ref[:, cols] if cols.start < half else cc_ref[:, cols.start - half : cols.stop - half]
        pre = conv_rows(ext, taps, rows, cols)
        prebc_ref[:, cols] = pre
        bc_ref[:, cols] = pre * sigmoid(pre)
    b_turned = split(jnp.transpose(bc_ref[:, 0:half]))
    for cols in tiles(width, 2 * LANES):
        cumx = cumx_ref[:, cols]
        weighted = jnp.exp(cumx[rows - 1 : rows] - cumx) * dtx_ref[:, cols] * x_out[:, cols]
        state_ref[:, cols] = diagonal_blocks(mul(b_turned, split(weighted)))


def inside_kernel(x_ref, bc_ref, cum_ref, cumt_ref, dtx_ref, skip_ref, y_ref, inner):
    rows, width = x_ref.shape
    half = GROUPS * STATE
    for g in range(GROUPS):
        own = slice(g * STATE, (g + 1) * STATE)
        c_g = split(bc_ref[:, half + g * STATE : half + (g + 1) * STATE])
        inner[g] = mul(c_g, split(bc_ref[:, own]), MT)
    causal = iota((rows, rows), 0) >= iota((rows, rows), 1)
    owner = lane_group(LANES)
    for r, cols in enumerate(tiles(width, LANES)):
        x = x_ref[:, cols]
        weighted = x * dtx_ref[:, cols]
        total = skip_ref[:, cols] * x
        for g in range(GROUPS):
            h = r * GROUPS + g
            gap = cum_ref[:, h : h + 1] - cumt_ref[h : h + 1, :]
            kernel = jnp.exp(jnp.where(causal, gap, -1e30)) * inner[g]
            total = total + mul(split(kernel), split(jnp.where(owner == g, weighted, 0.0)))
        y_ref[:, cols] = total


def forward_prefix(mine, states_ref, decays_ref, cols, count):
    total = jnp.zeros((STATE, cols.stop - cols.start), F32)

    def lap(j, total):
        return decays_ref[j, :, cols] * total + states_ref[j, :, cols]

    return lax.fori_loop(0, mine, lap, total)


def backward_prefix(mine, states_ref, decays_ref, cols, count):
    total = jnp.zeros((STATE, cols.stop - cols.start), F32)

    def lap(j, total):
        k = count - 1 - j
        return decays_ref[k, :, cols] * total + states_ref[k, :, cols]

    return lax.fori_loop(0, count - 1 - mine, lap, total)


def output_kernel(
    mine_ref, states_ref, decays_ref, y_ref, bc_ref, cumx_ref, z_ref, go_ref, gain_ref, y_out, enter_ref, sums_ref
):
    rows, width = y_ref.shape
    half = GROUPS * STATE
    count = states_ref.shape[0]
    c_all = split(bc_ref[:, half:])
    squares = jnp.zeros((rows, LANES), F32)
    inners = jnp.zeros((rows, LANES), F32)
    for cols in tiles(width, 2 * LANES):
        enter = forward_prefix(mine_ref[0], states_ref, decays_ref, cols, count)
        enter_ref[:, cols] = enter
        carried = mul(c_all, split(block_diagonal(enter)))
        y = y_ref[:, cols] + jnp.exp(cumx_ref[:, cols]) * carried
        y_out[:, cols] = y
        z = z_ref[:, cols].astype(F32)
        gated = y * (z * sigmoid(z))
        scaled = go_ref[:, cols].astype(F32) * gain_ref[:, cols]
        sq = gated * gated
        pr = scaled * gated
        squares = squares + sq[:, :LANES] + sq[:, LANES:]
        inners = inners + pr[:, :LANES] + pr[:, LANES:]
    pick = (iota((2 * GROUPS, LANES), 1) // HEAD_DIM).astype(jnp.int32)
    row = iota((2 * GROUPS, LANES), 0)
    sums_ref[...] = exact((pick == row).astype(F32), squares, MT) + exact(
        (pick + GROUPS == row).astype(F32), inners, MT
    )


def turn_kernel(
    group_width, sums_ref, y_ref, bc_ref, cumx_ref, z_ref, go_ref, gain_ref, dy_ref, dz_ref, gain_grad_ref, state_ref
):
    rows, width = y_ref.shape
    half = GROUPS * STATE
    turned = jnp.transpose(sums_ref[...])
    pick = iota((2 * GROUPS, LANES), 1) // HEAD_DIM
    row = iota((2 * GROUPS, LANES), 0)
    squares = exact(turned, (pick == row).astype(F32))
    inners = exact(turned, (pick + GROUPS == row).astype(F32))
    inverse = lax.rsqrt(squares / group_width + EPSILON)
    correction = inverse * inverse * inverse * inners / group_width
    inverse = jnp.concatenate([inverse, inverse], axis=1)
    correction = jnp.concatenate([correction, correction], axis=1)
    c_turned = split(jnp.transpose(bc_ref[:, half:]))
    for cols in tiles(width, 2 * LANES):
        y = y_ref[:, cols]
        z = z_ref[:, cols].astype(F32)
        s = sigmoid(z)
        gate = z * s
        gated = y * gate
        go = go_ref[:, cols].astype(F32)
        gain_grad_ref[:, cols] = jnp.sum(go * gated * inverse, axis=0, keepdims=True)
        gated_grad = inverse * (go * gain_ref[:, cols]) - gated * correction
        dy = gated_grad * gate
        dy_ref[:, cols] = dy
        dz_ref[:, cols] = (gated_grad * y * (s * (1.0 + z * (1.0 - s)))).astype(BF16)
        state_ref[:, cols] = diagonal_blocks(mul(c_turned, split(jnp.exp(cumx_ref[:, cols]) * dy)))


def inside_back_kernel(
    x_ref, bc_ref, cum_ref, cumt_ref, dtx_ref, cumx_ref, enter_ref, dy_ref, dxd_ref, dbc_ref, inner, inner_grad
):
    rows, width = x_ref.shape
    half = GROUPS * STATE
    for g in range(GROUPS):
        own = slice(g * STATE, (g + 1) * STATE)
        c_g = split(bc_ref[:, half + g * STATE : half + (g + 1) * STATE])
        inner[g] = mul(split(bc_ref[:, own]), c_g, MT)
    inner_grad[...] = jnp.zeros_like(inner_grad)
    causal = iota((rows, rows), 0) <= iota((rows, rows), 1)
    owner = lane_group(LANES)
    for r, cols in enumerate(tiles(width, LANES)):
        dy = dy_ref[:, cols]
        weighted = split(x_ref[:, cols] * dtx_ref[:, cols])
        total = jnp.zeros((rows, LANES), F32)
        for g in range(GROUPS):
            h = r * GROUPS + g
            gap = cumt_ref[h : h + 1, :] - cum_ref[:, h : h + 1]
            decay = jnp.exp(jnp.where(causal, gap, -1e30))
            own = split(jnp.where(owner == g, dy, 0.0))
            total = total + mul(split(decay * inner[g]), own)
            inner_grad[g] = inner_grad[g] + decay * mul(weighted, own, MT)
        dxd_ref[:, cols] = total
    dc = jnp.zeros((rows, half), F32)
    for cols in tiles(width, 2 * LANES):
        pushed = jnp.exp(cumx_ref[:, cols]) * dy_ref[:, cols]
        dc = dc + mul(split(pushed), split(block_diagonal(enter_ref[:, cols])), MT)
    for g in range(GROUPS):
        own = slice(g * STATE, (g + 1) * STATE)
        other = slice(half + g * STATE, half + (g + 1) * STATE)
        grad = inner_grad[g]
        dbc_ref[:, own] = mul(split(grad), split(bc_ref[:, other]))
        dbc_ref[:, other] = dc[:, own] + mul(split(jnp.transpose(grad)), split(bc_ref[:, own]))


def finish_kernel(
    mine_ref, states_ref, decays_ref, x_ref, prex_ref, bc_ref, dt_ref, dtraw_ref, bias_ref, alog_ref, skip_ref,
    dtx_ref, cumx_ref, enter_ref, y_ref, dy_ref, dxd_ref, dbc_ref, xraw_ref, halo_ref,
    dpre_ref, dbc_out, ddt_ref, convx_ref, small_ref, ext,
):
    rows, width = x_ref.shape
    half = GROUPS * STATE
    heads = dt_ref.shape[1]
    count = states_ref.shape[0]
    ext[0:HALO, :] = halo_ref[:, 0:width].astype(F32)
    ext[HALO:, :] = xraw_ref[...].astype(F32)
    b_all = split(bc_ref[:, 0:half])
    size = 2 * LANES
    db = jnp.zeros((rows, half), F32)
    cum_grad = jnp.zeros((rows, heads), F32)
    step_grad = jnp.zeros((rows, heads), F32)
    ends = jnp.zeros((1, heads), F32)
    skips = jnp.zeros((1, heads), F32)
    for cols in tiles(width, size):
        later = backward_prefix(mine_ref[0], states_ref, decays_ref, cols, count)
        wide = split(block_diagonal(later))
        cumx = cumx_ref[:, cols]
        end = cumx[rows - 1 : rows]
        fade = jnp.exp(end - cumx)
        x = x_ref[:, cols]
        dtx = dtx_ref[:, cols]
        dy = dy_ref[:, cols]
        weighted = x * dtx
        from_state = fade * mul(b_all, wide)
        db = db + mul(split(fade * weighted), wide, MT)
        dxd = dxd_ref[:, cols] + from_state
        skip = skip_ref[:, cols]
        dx = dtx * dxd + skip * dy
        spread = (
            (iota((heads, size), 1) + cols.start) // HEAD_DIM == iota((heads, size), 0)
        ).astype(F32)
        cum_grad = cum_grad + exact(dy * (y_ref[:, cols] - skip * x) - weighted * dxd, spread, MT)
        step_grad = step_grad + exact(x * dxd, spread, MT)
        end_cols = jnp.sum(weighted * from_state, axis=0, keepdims=True) + jnp.exp(end) * jnp.sum(
            later * enter_ref[:, cols], axis=0, keepdims=True
        )
        ends = ends + exact(jnp.broadcast_to(end_cols, (8, size)), spread, MT)[0:1]
        skip_cols = jnp.sum(dy * x, axis=0, keepdims=True)
        skips = skips + exact(jnp.broadcast_to(skip_cols, (8, size)), spread, MT)[0:1]
        dpre = dx * silu_slope(prex_ref[:, cols])
        dpre_ref[:, cols] = dpre
        for k in range(CONV):
            convx_ref[k : k + 1, cols] = jnp.sum(
                dpre * ext[HALO - 3 + k : HALO - 3 + k + rows, cols], axis=0, keepdims=True
            )
    dbc_out[:, 0:half] = dbc_ref[:, 0:half] + db
    dbc_out[:, half:] = dbc_ref[:, half:]
    triu = (iota((rows, rows), 0) <= iota((rows, rows), 1)).astype(F32)
    log_grad = exact(triu, cum_grad) + ends
    rate = jnp.exp(alog_ref[...])
    raw_grad = (step_grad - rate * log_grad) * sigmoid(dtraw_ref[...] + bias_ref[...])
    ddt_ref[...] = raw_grad
    small_ref[...] = jnp.zeros_like(small_ref)
    small_ref[0:1, :] = jnp.sum(raw_grad, axis=0, keepdims=True)
    small_ref[1:2, :] = jnp.sum(-rate * log_grad * dt_ref[...], axis=0, keepdims=True)
    small_ref[2:3, :] = skips


def shared_kernel(dbc_ref, prebc_ref, braw_ref, craw_ref, halo_ref, dpre_ref, conv_ref, ext):
    rows, width = dbc_ref.shape
    half = braw_ref.shape[1]
    ext[0:HALO, :] = halo_ref[:, halo_ref.shape[1] - width :].astype(F32)
    ext[HALO:, 0:half] = braw_ref[...].astype(F32)
    ext[HALO:, half:] = craw_ref[...].astype(F32)
    for cols in tiles(width, LANES):
        dpre = dbc_ref[:, cols] * silu_slope(prebc_ref[:, cols])
        dpre_ref[:, cols] = dpre
        for k in range(CONV):
            conv_ref[k : k + 1, cols] = jnp.sum(
                dpre * ext[HALO - 3 + k : HALO - 3 + k + rows, cols], axis=0, keepdims=True
            )


def settle_kernel(dx_ref, dbc_ref, nx_ref, nbc_ref, cx_ref, cb_ref, cc_ref, gx_ref, gb_ref, gc_ref, ext):
    rows, width = dx_ref.shape
    half = gb_ref.shape[1]
    for source, after, outs in (
        (dx_ref, nx_ref, ((gx_ref, cx_ref, 0),)),
        (dbc_ref, nbc_ref, ((gb_ref, cb_ref, 0), (gc_ref, cc_ref, half))),
    ):
        ext[0:rows, :] = source[...]
        ext[rows : rows + 8, :] = after[...]
        for out, taps, start in outs:
            for cols in tiles(out.shape[1], LANES):
                here = slice(start + cols.start, start + cols.stop)
                total = taps[0:1, cols] * ext[3 : 3 + rows, here]
                for k in range(1, CONV):
                    total = total + taps[k : k + 1, cols] * ext[3 - k : 3 - k + rows, here]
                out[:, cols] = total.astype(BF16)


def call(kernel, outs, scratch, *args, scalars=0):
    vmem = pl.BlockSpec(memory_space=pltpu.VMEM)
    smem = pl.BlockSpec(memory_space=pltpu.SMEM)
    return pl.pallas_call(
        kernel,
        out_shape=[jax.ShapeDtypeStruct(s, d) for s, d in outs],
        in_specs=[smem] * scalars + [vmem] * (len(args) - scalars),
        out_specs=[vmem] * len(outs),
        scratch_shapes=[pltpu.VMEM(s, F32) for s in scratch],
        compiler_params=pltpu.CompilerParams(vmem_limit_bytes=48 * 1024 * 1024),
    )(*args)


def body(
    x_raw, b_raw, c_raw, z_gate, dt_raw, conv_x, conv_b, conv_c, dt_bias, a_log, d_skip, gain, grad_out
):
    rows, width = x_raw.shape
    heads = dt_raw.shape[1]
    half = b_raw.shape[1]
    count = lax.axis_size("ctx")
    mine = lax.axis_index("ctx").astype(jnp.int32).reshape(1)
    group_width = width * lax.axis_size("tp") // GROUPS
    bias, alog, gain_row = dt_bias[None], a_log[None], gain[None]
    skip = jnp.repeat(d_skip, HEAD_DIM)[None]
    tails = jnp.concatenate([x_raw[rows - HALO :], b_raw[rows - HALO :], c_raw[rows - HALO :]], axis=1)
    halo = lax.ppermute(tails, "ctx", [(i, i + 1) for i in range(count - 1)])
    full = ((rows, width), F32)
    shared = ((rows, 2 * half), F32)
    prex, x, prebc, bc, step, cum, cumt, dtx, cumx, own, dec = call(
        begin_kernel,
        [full, full, shared, shared, ((rows, heads), F32), ((rows, heads), F32), ((heads, rows), F32), full, full,
         ((STATE, width), F32), ((1, width), F32)],
        [(HALO + rows, width)],
        x_raw, b_raw, c_raw, halo, dt_raw, conv_x, conv_b, conv_c, bias, alog,
    )
    states = lax.all_gather(own, "ctx")
    decays = lax.all_gather(dec, "ctx")
    (y_own,) = call(inside_kernel, [full], [(GROUPS, rows, rows)], x, bc, cum, cumt, dtx, skip)
    y, enter, sums = call(
        output_kernel,
        [full, ((STATE, width), F32), ((2 * GROUPS, rows), F32)],
        [],
        mine, states, decays, y_own, bc, cumx, z_gate, grad_out, gain_row,
        scalars=1,
    )
    sums = lax.psum(sums, "tp")
    dy, dz, gain_part, state_part = call(
        functools.partial(turn_kernel, group_width),
        [full, ((rows, width), BF16), ((1, width), F32), ((STATE, width), F32)],
        [],
        sums, y, bc, cumx, z_gate, grad_out, gain_row,
    )
    state_grads = lax.all_gather(state_part, "ctx")
    dxd, dbc = call(
        inside_back_kernel,
        [full, shared],
        [(GROUPS, rows, rows), (GROUPS, rows, rows)],
        x, bc, cum, cumt, dtx, cumx, enter, dy,
    )
    dprex, dbc, ddt, convx_part, small = call(
        finish_kernel,
        [full, shared, ((rows, heads), F32), ((CONV, width), F32), ((8, heads), F32)],
        [(HALO + rows, width)],
        mine, state_grads, decays, x, prex, bc, step, dt_raw, bias, alog, skip,
        dtx, cumx, enter, y, dy, dxd, dbc, x_raw, halo,
        scalars=1,
    )
    back = [(i + 1, i) for i in range(count - 1)]
    next_x = lax.ppermute(dprex[:8], "ctx", back)
    dbc = lax.psum(dbc, "tp")
    dprebc, convbc_part = call(
        shared_kernel,
        [shared, ((CONV, 2 * half), F32)],
        [(HALO + rows, 2 * half)],
        dbc, prebc, b_raw, c_raw, halo,
    )
    next_bc = lax.ppermute(dprebc[:8], "ctx", back)
    packed = jnp.concatenate(
        [convx_part, convbc_part, gain_part, jnp.pad(small[:3].reshape(1, -1), ((0, 0), (0, width - 3 * heads)))], axis=0
    )
    packed = lax.psum(packed, "ctx")
    gx, gb, gc = call(
        settle_kernel,
        [((rows, width), BF16), ((rows, half), BF16), ((rows, half), BF16)],
        [(rows + 8, width)],
        dprex, dprebc, next_x, next_bc, conv_x, conv_b, conv_c,
    )
    last = packed[9]
    return (
        gx, gb, gc, dz, ddt,
        packed[0:4], packed[4:8, :half], packed[4:8, half:],
        last[:heads], last[heads : 2 * heads], last[2 * heads : 3 * heads], packed[8],
    )


def solution(mesh):
    col, row, cut = P("ctx", "tp"), P("ctx", None), P("tp")
    return jax.shard_map(
        body,
        mesh=mesh,
        in_specs=(col, row, row, col, col, P(None, "tp"), P(), P(), cut, cut, cut, cut, col),
        out_specs=(col, row, row, col, col, P(None, "tp"), P(), P(), cut, cut, cut, cut),
        check_vma=False,
    )
```

```python
import jax
import jax.numpy as jnp
from jax import lax
from jax.experimental import pallas as pl
from jax.experimental.pallas import tpu as pltpu
from jax.sharding import PartitionSpec as P

HEAD_DIM = 32
STATE = 128
GROUPS = 4
CONV = 4
HALO = 16
LANES = 128
EPSILON = 1e-05
F32 = jnp.float32
BF16 = jnp.bfloat16
MM = ((1,), (0,))
MT = ((1,), (1,))


def split(value):
    high = value.astype(BF16)
    return high, (value - high.astype(F32)).astype(BF16)


def mul(a, b, dims=MM):
    def dot(u, v):
        return lax.dot_general(u, v, (dims, ((), ())), preferred_element_type=F32)

    return dot(a[0], b[0]) + (dot(a[0], b[1]) + dot(a[1], b[0]))


def exact(a, b, dims=MM):
    return lax.dot_general(
        a, b, (dims, ((), ())), preferred_element_type=F32, precision=lax.Precision.HIGHEST
    )


def sigmoid(v):
    return 1.0 / (1.0 + jnp.exp(-v))


def silu_slope(v):
    s = sigmoid(v)
    return s * (1.0 + v * (1.0 - s))


def iota(shape, axis):
    return lax.broadcasted_iota(jnp.int32, shape, axis)


def lane_group(width):
    return (iota((1, width), 1) // HEAD_DIM) % GROUPS


def head_spread(heads, width):
    return (iota((heads, width), 1) // HEAD_DIM == iota((heads, width), 0)).astype(F32)


def block_diagonal(state):
    owner = lane_group(state.shape[1])
    return jnp.concatenate([jnp.where(owner == g, state, 0.0) for g in range(GROUPS)], axis=0)


def diagonal_blocks(stacked):
    owner = lane_group(stacked.shape[1])
    total = jnp.zeros((STATE, stacked.shape[1]), F32)
    for g in range(GROUPS):
        total = jnp.where(owner == g, stacked[g * STATE : (g + 1) * STATE], total)
    return total


def tiles(width, size):
    return [slice(i, i + size) for i in range(0, width, size)]


def conv_rows(ext, taps, rows, cols):
    total = taps[0:1, :] * ext[HALO - 3 : HALO - 3 + rows, cols]
    for k in range(1, CONV):
        total = total + taps[k : k + 1, :] * ext[HALO - 3 + k : HALO - 3 + k + rows, cols]
    return total

MESH = pl.DeviceIdType.MESH
ROW_F = STATE + 8


def pair(ref, cols):
    first = cols.start // LANES
    return jnp.concatenate([ref[first], ref[first + 1]], axis=1)


def mixer_kernel(
    x_hbm, b_hbm, c_hbm, z_hbm, dtt_hbm, cx_hbm, cb_hbm, cc_hbm, bias_hbm, alog_hbm, dskip_hbm, gain_hbm, go_hbm,
    gx_hbm, gb_hbm, gc_hbm, dz_hbm, ddt_hbm, convx_hbm, convb_hbm, convc_hbm, small_hbm,
    x_in, bc_in, z_ref, dtt_ref, cx_ref, cbc_ref, bias_ref, alog_ref, dskip_ref, gain_ref, go_ref,
    halo_ref, extx, extbc, prex_ref, x_ref, prebc_ref, bc_ref, cumt_ref, dtx_ref, cumx_ref, skip_ref,
    y_ref, dy_ref, dxd_ref, inner, inner_grad,
    own_f, slots_f, outs_f, enter_ref, own_b, slots_b, outs_b, later_ref,
    own_p, slots_p, outs_p, total_p,
    sums_slots, early, slots_e, late, slots_l, final, taps_all, dpre_own, next_x, next_bc,
    gx_ref, gbc_ref, dz_ref, ddt_ref, convbc_ref, small_ref,
    load_sem, store_sem, ctx_send, ctx_recv, tp_send, tp_recv, halo_send, halo_recv,
):
    me, tp = lax.axis_index("ctx"), lax.axis_index("tp")
    count, lanes_of_heads = lax.axis_size("ctx"), lax.axis_size("tp")
    ranks = lanes_of_heads
    rows, width = x_in.shape
    half = GROUPS * STATE
    heads = dtt_ref.shape[0]
    parts = width // LANES
    stride = count // parts
    my_part = me // stride
    size = 2 * LANES

    loads = []

    def load(src, dst):
        copy = pltpu.make_async_copy(src, dst, load_sem.at[len(loads)])
        copy.start()
        loads.append(copy)

    load(x_hbm, x_in)
    load(b_hbm, bc_in.at[:, 0:half])
    load(c_hbm, bc_in.at[:, half:])
    load(dtt_hbm, dtt_ref)
    load(cx_hbm, cx_ref)
    load(cb_hbm, cbc_ref.at[:, 0:half])
    load(cc_hbm, cbc_ref.at[:, half:])
    load(bias_hbm, bias_ref)
    load(alog_hbm, alog_ref)
    load(dskip_hbm, dskip_ref)
    load(gain_hbm, gain_ref)
    load(z_hbm, z_ref)
    load(go_hbm, go_ref)

    barrier = pltpu.get_barrier_semaphore()
    for d in range(1, count):
        pl.semaphore_signal(barrier, inc=1, device_id=(lax.rem(me + d, count), tp), device_id_type=MESH)
    for d in range(1, ranks):
        pl.semaphore_signal(barrier, inc=1, device_id=(me, lax.rem(tp + d, ranks)), device_id_type=MESH)
    pl.semaphore_wait(barrier, count - 1 + ranks - 1)

    def remote(src, dst, send, recv, ctx, rank):
        return pltpu.make_async_remote_copy(
            src_ref=src, dst_ref=dst, send_sem=send, recv_sem=recv, device_id=(ctx, rank), device_id_type=MESH
        )

    ahead, behind = lax.rem(me + 1, count), lax.rem(me + count - 1, count)
    for copy in loads[0:3]:
        copy.wait()
    tail = [
        remote(x_in.at[rows - HALO :, :], halo_ref.at[:, 0:width], halo_send.at[0], halo_recv.at[0], ahead, tp),
        remote(bc_in.at[rows - HALO :, :], halo_ref.at[:, width:], halo_send.at[1], halo_recv.at[1], ahead, tp),
    ]

    @pl.when(me < count - 1)
    def _():
        for copy in tail:
            copy.start()

    for copy in loads[3:11]:
        copy.wait()

    step = jax.nn.softplus(jnp.transpose(dtt_ref[...]) + bias_ref[...])
    rate = jnp.exp(alog_ref[...])
    tril = (iota((rows, rows), 0) >= iota((rows, rows), 1)).astype(F32)
    cum = exact(tril, -rate * step)
    cumt_ref[...] = jnp.transpose(cum)
    spread = head_spread(heads, width)
    dtx_ref[...] = exact(step, spread)
    cumx_ref[...] = exact(cum, spread)
    skip_ref[...] = exact(jnp.broadcast_to(dskip_ref[...], (8, heads)), spread)
    extx[HALO:, :] = x_in[...].astype(F32)
    extbc[HALO:, :] = bc_in[...].astype(F32)

    @pl.when(me == 0)
    def _():
        extx[0:HALO, :] = jnp.zeros((HALO, width), F32)
        extbc[0:HALO, :] = jnp.zeros((HALO, 2 * half), F32)

    @pl.when(me > 0)
    def _():
        for copy in tail:
            copy.wait_recv()
        extx[0:HALO, :] = halo_ref[:, 0:width].astype(F32)
        extbc[0:HALO, :] = halo_ref[:, width:].astype(F32)

    for cols in tiles(2 * half, LANES):
        pre = conv_rows(extbc, cbc_ref[:, cols], rows, cols)
        prebc_ref[:, cols] = pre
        bc_ref[:, cols] = pre * sigmoid(pre)
    for cols in tiles(width, LANES):
        pre = conv_rows(extx, cx_ref[:, cols], rows, cols)
        prex_ref[:, cols] = pre
        x_ref[:, cols] = pre * sigmoid(pre)
    b_turned = split(jnp.transpose(bc_ref[:, 0:half]))
    for cols in tiles(width, size):
        cumx = cumx_ref[:, cols]
        end = cumx[rows - 1 : rows]
        weighted = jnp.exp(end - cumx) * dtx_ref[:, cols] * x_ref[:, cols]
        state = diagonal_blocks(mul(b_turned, split(weighted)))
        decay = jnp.broadcast_to(jnp.exp(end), (8, size))
        for i in range(2):
            own_f[cols.start // LANES + i, 0:STATE, :] = state[:, i * LANES : (i + 1) * LANES]
            own_f[cols.start // LANES + i, STATE:, :] = decay[:, i * LANES : (i + 1) * LANES]

    def to_owner(own, slots, k, part):
        return remote(own.at[part], slots.at[me], ctx_send.at[k, part], ctx_recv.at[k, me], part * stride, tp)

    def gather_tiles(own, slots, k):
        for d in range(1, parts):
            to_owner(own, slots, k, lax.rem(my_part + d, parts)).start()
        if stride > 1:
            @pl.when(lax.rem(me, stride) != 0)
            def _():
                to_owner(own, slots, k, my_part).start()

    def owner_only(act):
        if stride > 1:
            pl.when(lax.rem(me, stride) == 0)(act)
        else:
            act()

    def from_owner(out, result, k, i):
        return remote(out, result.at[my_part], ctx_send.at[k + 1, i], ctx_recv.at[k + 1, my_part], i, tp)

    def slot_wait(slots, k, j):
        @pl.when(j != me)
        def _():
            remote(slots.at[j], slots.at[j], ctx_send.at[k, 0], ctx_recv.at[k, j], ahead, tp).wait_recv()

    def settle_exchange(own, slots, outs, result, k):
        for j in range(parts):
            @pl.when(me != j * stride)
            def _():
                remote(result.at[j], result.at[j], ctx_send.at[k + 1, 0], ctx_recv.at[k + 1, j], ahead, tp).wait_recv()

    def drain(own, slots, outs, result, k):
        for j in range(parts):
            @pl.when(me != j * stride)
            def _():
                to_owner(own, slots, k, j).wait_send()

        def sent():
            for i in range(count):
                @pl.when(me != i)
                def _():
                    from_owner(outs.at[i], result, k, i).wait_send()

        owner_only(sent)

    def scan(own, slots, decays, outs, result, k, order):
        def act():
            slots[me] = own[my_part]
            total = jnp.zeros((STATE, LANES), F32)
            for i in order:
                outs[i] = total

                @pl.when(i != me)
                def _():
                    from_owner(outs.at[i], result, k, i).start()

                slot_wait(slots, k, i)
                total = decays[i, STATE : STATE + 1, :] * total + slots[i, 0:STATE, :]
            result[my_part] = outs[me]

        owner_only(act)

    gather_tiles(own_f, slots_f, 0)

    owner = lane_group(LANES)
    causal = iota((rows, rows), 0) >= iota((rows, rows), 1)
    for g in range(GROUPS):
        c_g = split(bc_ref[:, half + g * STATE : half + (g + 1) * STATE])
        inner[g] = mul(c_g, split(bc_ref[:, g * STATE : (g + 1) * STATE]), MT)
    for r, cols in enumerate(tiles(width, LANES)):
        x = x_ref[:, cols]
        weighted = x * dtx_ref[:, cols]
        cumx = cumx_ref[:, cols]
        total = skip_ref[0:1, cols] * x
        for g in range(GROUPS):
            h = r * GROUPS + g
            gap = cumx[:, g * HEAD_DIM : g * HEAD_DIM + 1] - cumt_ref[h : h + 1, :]
            fade = jnp.exp(jnp.where(causal, gap, -1e30)) * inner[g]
            total = total + mul(split(fade), split(jnp.where(owner == g, weighted, 0.0)))
        y_ref[:, cols] = total

    scan(own_f, slots_f, slots_f, outs_f, enter_ref, 0, range(count))
    for copy in loads[11:]:
        copy.wait()
    settle_exchange(own_f, slots_f, outs_f, enter_ref, 0)

    c_all = split(bc_ref[:, half:])
    squares = jnp.zeros((rows, LANES), F32)
    inners = jnp.zeros((rows, LANES), F32)
    for cols in tiles(width, size):
        carried = mul(c_all, split(block_diagonal(pair(enter_ref, cols))))
        y = y_ref[:, cols] + jnp.exp(cumx_ref[:, cols]) * carried
        y_ref[:, cols] = y
        z = z_ref[:, cols].astype(F32)
        gated = y * (z * sigmoid(z))
        scaled = go_ref[:, cols].astype(F32) * gain_ref[:, cols]
        sq = gated * gated
        pr = scaled * gated
        squares = squares + sq[:, :LANES] + sq[:, LANES:]
        inners = inners + pr[:, :LANES] + pr[:, LANES:]
    pick = iota((2 * GROUPS, LANES), 1) // HEAD_DIM
    row = iota((2 * GROUPS, LANES), 0)
    pick_low = (pick == row).astype(F32)
    pick_high = (pick + GROUPS == row).astype(F32)
    sums_slots[tp] = exact(pick_low, squares, MT) + exact(pick_high, inners, MT)

    def tp_copies(own_at, dst_at, k):
        return [
            remote(own_at(q), dst_at, tp_send.at[k, q], tp_recv.at[k, tp], me, q)
            for q in [lax.rem(tp + d, ranks) for d in range(1, ranks)]
        ]

    def tp_wait(slots, k):
        for d in range(1, ranks):
            q = lax.rem(tp + d, ranks)
            remote(slots.at[q], slots.at[q], tp_send.at[k, q], tp_recv.at[k, q], me, q).wait_recv()

    started = []

    def tp_start(own_at, dst_at, k):
        copies = tp_copies(own_at, dst_at, k)
        for copy in copies:
            copy.start()
        started.extend(copies)

    tp_start(lambda q: sums_slots.at[tp], sums_slots.at[tp], 0)
    tp_wait(sums_slots, 0)
    sums = sums_slots[0]
    for q in range(1, ranks):
        sums = sums + sums_slots[q]
    group_width = width * ranks // GROUPS
    turned = jnp.transpose(sums)
    inverse = lax.rsqrt(exact(turned, pick_low) / group_width + EPSILON)
    correction = inverse * inverse * inverse * exact(turned, pick_high) / group_width
    inverse = jnp.concatenate([inverse, inverse], axis=1)
    correction = jnp.concatenate([correction, correction], axis=1)
    c_turned = split(jnp.transpose(bc_ref[:, half:]))
    own_p[...] = jnp.zeros_like(own_p)
    for cols in tiles(width, size):
        y = y_ref[:, cols]
        z = z_ref[:, cols].astype(F32)
        s = sigmoid(z)
        gate = z * s
        gated = y * gate
        go = go_ref[:, cols].astype(F32)
        gain_grad = jnp.sum(go * gated * inverse, axis=0, keepdims=True)
        gated_grad = inverse * (go * gain_ref[:, cols]) - gated * correction
        dy = gated_grad * gate
        dy_ref[:, cols] = dy
        dz_ref[:, cols] = (gated_grad * y * (s * (1.0 + z * (1.0 - s)))).astype(BF16)
        state = diagonal_blocks(mul(c_turned, split(jnp.exp(cumx_ref[:, cols]) * dy)))
        for i in range(2):
            part = slice(i * LANES, (i + 1) * LANES)
            own_b[cols.start // LANES + i] = state[:, part]
            own_p[cols.start // LANES + i, 4:5, :] = gain_grad[:, part]
    gather_tiles(own_b, slots_b, 2)

    stores = []

    def store(src, dst):
        copy = pltpu.make_async_copy(src, dst, store_sem.at[len(stores)])
        copy.start()
        stores.append(copy)

    store(dz_ref, dz_hbm)

    for g in range(GROUPS):
        c_g = split(bc_ref[:, half + g * STATE : half + (g + 1) * STATE])
        inner[g] = mul(split(bc_ref[:, g * STATE : (g + 1) * STATE]), c_g, MT)
    inner_grad[...] = jnp.zeros_like(inner_grad)
    causal = iota((rows, rows), 0) <= iota((rows, rows), 1)
    for r, cols in enumerate(tiles(width, LANES)):
        dy = dy_ref[:, cols]
        cumx = cumx_ref[:, cols]
        weighted = split(x_ref[:, cols] * dtx_ref[:, cols])
        total = jnp.zeros((rows, LANES), F32)
        for g in range(GROUPS):
            h = r * GROUPS + g
            gap = cumt_ref[h : h + 1, :] - cumx[:, g * HEAD_DIM : g * HEAD_DIM + 1]
            decay = jnp.exp(jnp.where(causal, gap, -1e30))
            masked = split(jnp.where(owner == g, dy, 0.0))
            total = total + mul(split(decay * inner[g]), masked)
            inner_grad[g] = inner_grad[g] + decay * mul(weighted, masked, MT)
        dxd_ref[:, cols] = total
    dc = jnp.zeros((rows, half), F32)
    for cols in tiles(width, size):
        pushed = jnp.exp(cumx_ref[:, cols]) * dy_ref[:, cols]
        dc = dc + mul(split(pushed), split(block_diagonal(pair(enter_ref, cols))), MT)
    for g in range(GROUPS):
        own = slice(g * STATE, (g + 1) * STATE)
        other = slice(half + g * STATE, half + (g + 1) * STATE)
        grad = inner_grad[g]
        early[g, 0:rows, :] = mul(split(grad), split(bc_ref[:, other]))
        early[g, rows:, :] = dc[:, own] + mul(split(jnp.transpose(grad)), split(bc_ref[:, own]))
    tp_start(lambda q: early.at[q], slots_e.at[tp], 1)

    scan(own_b, slots_b, slots_f, outs_b, later_ref, 2, range(count - 1, -1, -1))
    settle_exchange(own_b, slots_b, outs_b, later_ref, 2)

    db = jnp.zeros((rows, half), F32)
    for cols in tiles(width, size):
        wide = split(block_diagonal(pair(later_ref, cols)))
        cumx = cumx_ref[:, cols]
        fade = jnp.exp(cumx[rows - 1 : rows] - cumx)
        db = db + mul(split(fade * (x_ref[:, cols] * dtx_ref[:, cols])), wide, MT)
    for g in range(GROUPS):
        late[g] = db[:, g * STATE : (g + 1) * STATE]
    tp_start(lambda q: late.at[q], slots_l.at[tp], 2)

    b_all = split(bc_ref[:, 0:half])
    cum_grad = jnp.zeros((rows, heads), F32)
    step_grad = jnp.zeros((rows, heads), F32)
    ends = jnp.zeros((8, heads), F32)
    skips = jnp.zeros((8, heads), F32)
    for cols in tiles(width, size):
        later = pair(later_ref, cols)
        cumx = cumx_ref[:, cols]
        end = cumx[rows - 1 : rows]
        x = x_ref[:, cols]
        dtx = dtx_ref[:, cols]
        dy = dy_ref[:, cols]
        weighted = x * dtx
        from_state = jnp.exp(end - cumx) * mul(b_all, split(block_diagonal(later)))
        dxd = dxd_ref[:, cols] + from_state
        skip = skip_ref[0:1, cols]
        dx = dtx * dxd + skip * dy
        spread = ((iota((heads, size), 1) + cols.start) // HEAD_DIM == iota((heads, size), 0)).astype(F32)
        cum_grad = cum_grad + exact(dy * (y_ref[:, cols] - skip * x) - weighted * dxd, spread, MT)
        step_grad = step_grad + exact(x * dxd, spread, MT)
        end_cols = jnp.sum(weighted * from_state, axis=0, keepdims=True) + jnp.exp(end) * jnp.sum(
            later * pair(enter_ref, cols), axis=0, keepdims=True
        )
        ends = ends + exact(jnp.broadcast_to(end_cols, (8, size)), spread, MT)
        skip_cols = jnp.sum(dy * x, axis=0, keepdims=True)
        skips = skips + exact(jnp.broadcast_to(skip_cols, (8, size)), spread, MT)
        dpre = dx * silu_slope(prex_ref[:, cols])
        dxd_ref[:, cols] = dpre
        for k in range(CONV):
            tap = jnp.sum(dpre * extx[HALO - 3 + k : HALO - 3 + k + rows, cols], axis=0, keepdims=True)
            for i in range(2):
                own_p[cols.start // LANES + i, k : k + 1, :] = tap[:, i * LANES : (i + 1) * LANES]
    send_x = remote(dxd_ref.at[0:8, :], next_x, halo_send.at[2], halo_recv.at[2], behind, tp)

    @pl.when(me > 0)
    def _():
        send_x.start()

    triu = (iota((rows, rows), 0) <= iota((rows, rows), 1)).astype(F32)
    log_grad = exact(triu, cum_grad) + ends[0:1]
    raw_grad = (step_grad - rate * log_grad) * sigmoid(jnp.transpose(dtt_ref[...]) + bias_ref[...])
    ddt_ref[...] = jnp.transpose(raw_grad)
    store(ddt_ref, ddt_hbm)
    small = [
        jnp.sum(raw_grad, axis=0, keepdims=True),
        jnp.sum(-rate * log_grad * step, axis=0, keepdims=True),
        skips[0:1],
    ]
    for i in range(3):
        own_p[i, 5:6, 0:heads] = small[i]

    tp_wait(slots_e, 1)
    tp_wait(slots_l, 2)
    slots_e[tp] = early[tp]
    slots_l[tp] = late[tp]
    both = slots_e[0]
    db = slots_l[0]
    for q in range(1, ranks):
        both = both + slots_e[q]
        db = db + slots_l[q]
    for i, grad in ((0, both[0:rows] + db), (1, both[rows:])):
        mine = pl.ds(pl.multiple_of(i * half + tp * LANES, LANES), LANES)
        dpre = grad * silu_slope(prebc_ref[:, mine])
        dpre_own[i, 0:rows, :] = dpre
        for k in range(CONV):
            own_p[i * CONV + k, 6:7, :] = jnp.sum(
                dpre * extbc[HALO - 3 + k : HALO - 3 + k + rows, mine], axis=0, keepdims=True
            )
    send_bc = remote(dpre_own.at[:, 0:8, :], next_bc, halo_send.at[3], halo_recv.at[3], behind, tp)

    @pl.when(me > 0)
    def _():
        send_bc.start()

    gather_tiles(own_p, slots_p, 4)

    extx[0:rows, :] = dxd_ref[...]

    @pl.when(me < count - 1)
    def _():
        send_x.wait_recv()
        extx[rows : rows + 8, :] = next_x[...]

    @pl.when(me == count - 1)
    def _():
        extx[rows : rows + 8, :] = jnp.zeros((8, width), F32)

    for cols in tiles(width, LANES):
        total = cx_ref[0:1, cols] * extx[3 : 3 + rows, cols]
        for k in range(1, CONV):
            total = total + cx_ref[k : k + 1, cols] * extx[3 - k : 3 - k + rows, cols]
        gx_ref[:, cols] = total.astype(BF16)
    store(gx_ref, gx_hbm)

    def sum_parts():
        slots_p[me] = own_p[my_part]
        for j in range(count):
            slot_wait(slots_p, 4, j)
        total = slots_p[0]
        for j in range(1, count):
            total = total + slots_p[j]
        outs_p[0] = total
        for d in range(1, count):
            from_owner(outs_p.at[0], total_p, 4, lax.rem(me + d, count)).start()
        total_p[my_part] = total

    owner_only(sum_parts)

    @pl.when(me < count - 1)
    def _():
        send_bc.wait_recv()
        dpre_own[:, rows : rows + 8, :] = next_bc[...]

    @pl.when(me == count - 1)
    def _():
        dpre_own[:, rows : rows + 8, :] = jnp.zeros((2, 8, LANES), F32)

    for i in range(2):
        taps = cbc_ref[:, pl.ds(pl.multiple_of(i * half + tp * LANES, LANES), LANES)]
        total = taps[0:1] * dpre_own[i, 3 : 3 + rows, :]
        for k in range(1, CONV):
            total = total + taps[k : k + 1] * dpre_own[i, 3 - k : 3 - k + rows, :]
        final[tp, i * rows : (i + 1) * rows, :] = total.astype(BF16)
    tp_start(lambda q: final.at[tp], final.at[tp], 3)

    settle_exchange(own_p, slots_p, outs_p, total_p, 4)
    for i in range(2 * CONV):
        taps_all[tp, i : i + 1, :] = total_p[i, 6:7, :]
    tp_start(lambda q: taps_all.at[tp], taps_all.at[tp], 4)
    for r, cols in enumerate(tiles(width, LANES)):
        small_ref[:, cols] = total_p[r]
    store(small_ref.at[0:4, :], convx_hbm)
    store(small_ref, small_hbm)

    tp_wait(final, 3)
    for q in range(ranks):
        for i in range(2):
            gbc_ref[i, :, q * STATE : (q + 1) * STATE] = final[q, i * rows : (i + 1) * rows, :]
    store(gbc_ref.at[0], gb_hbm)
    store(gbc_ref.at[1], gc_hbm)
    tp_wait(taps_all, 4)
    for q in range(ranks):
        for i in range(2):
            convbc_ref[i, :, q * STATE : (q + 1) * STATE] = taps_all[q, i * CONV : (i + 1) * CONV, :]
    store(convbc_ref.at[0], convb_hbm)
    store(convbc_ref.at[1], convc_hbm)

    @pl.when(me < count - 1)
    def _():
        for copy in tail:
            copy.wait_send()

    @pl.when(me > 0)
    def _():
        send_x.wait_send()
        send_bc.wait_send()

    drain(own_f, slots_f, outs_f, enter_ref, 0)
    drain(own_b, slots_b, outs_b, later_ref, 2)
    drain(own_p, slots_p, outs_p, total_p, 4)
    for copy in started:
        copy.wait_send()
    for copy in stores:
        copy.wait()


def body(
    x_raw, b_raw, c_raw, z_gate, dt_raw, conv_x, conv_b, conv_c, dt_bias, a_log, d_skip, gain, grad_out
):
    rows, width = x_raw.shape
    heads = dt_raw.shape[1]
    half = b_raw.shape[1]
    count, ranks = lax.axis_size("ctx"), lax.axis_size("tp")
    parts = width // LANES
    hbm = pl.BlockSpec(memory_space=pl.ANY)

    def f32(*shape):
        return pltpu.VMEM(shape, F32)

    def b16(*shape):
        return pltpu.VMEM(shape, BF16)

    full, shared = f32(rows, width), f32(rows, 2 * half)
    outs = [
        ((rows, width), BF16), ((rows, half), BF16), ((rows, half), BF16), ((rows, width), BF16), ((heads, rows), F32),
        ((CONV, width), F32), ((CONV, half), F32), ((CONV, half), F32), ((8, width), F32),
    ]
    scratch = [
        b16(rows, width), b16(rows, 2 * half), b16(rows, width), f32(heads, rows), f32(CONV, width),
        f32(CONV, 2 * half), f32(1, heads), f32(1, heads), f32(1, heads), f32(1, width), b16(rows, width),
        b16(HALO, width + 2 * half), f32(HALO + rows, width), f32(HALO + rows, 2 * half), full, full, shared, shared,
        f32(heads, rows), full, full, f32(8, width),
        full, full, full, f32(GROUPS, rows, rows), f32(GROUPS, rows, rows),
        f32(parts, ROW_F, LANES), f32(count, ROW_F, LANES), f32(count, STATE, LANES), f32(parts, STATE, LANES),
        f32(parts, STATE, LANES), f32(count, STATE, LANES), f32(count, STATE, LANES), f32(parts, STATE, LANES),
        f32(parts, 8, LANES), f32(count, 8, LANES), f32(count, 8, LANES), f32(parts, 8, LANES),
        f32(ranks, 8, rows), f32(ranks, 2 * rows, LANES), f32(ranks, 2 * rows, LANES), f32(ranks, rows, LANES),
        f32(ranks, rows, LANES), b16(ranks, 2 * rows, LANES), f32(ranks, 8, LANES), f32(2, rows + 8, LANES),
        f32(8, width), f32(2, 8, LANES),
        b16(rows, width), b16(2, rows, half), b16(rows, width), f32(heads, rows), f32(2, CONV, half), f32(8, width),
    ] + [
        pltpu.SemaphoreType.DMA(s)
        for s in ((13,), (10,), (6, count), (6, count), (5, ranks), (5, ranks), (4,), (4,))
    ]
    gx, gb, gc, dz, ddt, convx, convb, convc, small = pl.pallas_call(
        mixer_kernel,
        out_shape=[jax.ShapeDtypeStruct(s, d) for s, d in outs],
        in_specs=[hbm] * 13,
        out_specs=[hbm] * len(outs),
        scratch_shapes=scratch,
        compiler_params=pltpu.CompilerParams(
            collective_id=0, has_side_effects=True, vmem_limit_bytes=56 * 1024 * 1024
        ),
    )(
        x_raw, b_raw, c_raw, z_gate, dt_raw.T, conv_x, conv_b, conv_c, dt_bias[None], a_log[None], d_skip[None],
        gain[None], grad_out,
    )
    return (
        gx, gb, gc, dz, ddt.T, convx, convb, convc,
        small[5, :heads], small[5, LANES : LANES + heads], small[5, 2 * LANES : 2 * LANES + heads], small[4],
    )


def solution(mesh):
    col, row, cut = P("ctx", "tp"), P("ctx", None), P("tp")
    return jax.shard_map(
        body,
        mesh=mesh,
        in_specs=(col, row, row, col, col, P(None, "tp"), P(), P(), cut, cut, cut, cut, col),
        out_specs=(col, row, row, col, col, P(None, "tp"), P(), P(), cut, cut, cut, cut),
        check_vma=False,
    )
```

```python
import jax
import jax.numpy as jnp
from jax import lax
from jax.experimental import pallas as pl
from jax.experimental.pallas import tpu as pltpu
from jax.sharding import PartitionSpec as P

HEAD_DIM = 32
STATE = 128
GROUPS = 4
CONV = 4
HALO = 16
LANES = 128
EPSILON = 1e-05
F32 = jnp.float32
BF16 = jnp.bfloat16
MM = ((1,), (0,))
MT = ((1,), (1,))


def split(value):
    high = value.astype(BF16)
    return high, (value - high.astype(F32)).astype(BF16)


def mul(a, b, dims=MM):
    def dot(u, v):
        return lax.dot_general(u, v, (dims, ((), ())), preferred_element_type=F32)

    return dot(a[0], b[0]) + (dot(a[0], b[1]) + dot(a[1], b[0]))


def exact(a, b, dims=MM):
    return lax.dot_general(
        a, b, (dims, ((), ())), preferred_element_type=F32, precision=lax.Precision.HIGHEST
    )


def sigmoid(v):
    return 1.0 / (1.0 + jnp.exp(-v))


def silu_slope(v):
    s = sigmoid(v)
    return s * (1.0 + v * (1.0 - s))


def iota(shape, axis):
    return lax.broadcasted_iota(jnp.int32, shape, axis)


def lane_group(width):
    return (iota((1, width), 1) // HEAD_DIM) % GROUPS


def head_spread(heads, width):
    return (iota((heads, width), 1) // HEAD_DIM == iota((heads, width), 0)).astype(F32)


def block_diagonal(state):
    owner = lane_group(state.shape[1])
    return jnp.concatenate([jnp.where(owner == g, state, 0.0) for g in range(GROUPS)], axis=0)


def diagonal_blocks(stacked):
    owner = lane_group(stacked.shape[1])
    total = jnp.zeros((STATE, stacked.shape[1]), F32)
    for g in range(GROUPS):
        total = jnp.where(owner == g, stacked[g * STATE : (g + 1) * STATE], total)
    return total


def tiles(width, size):
    return [slice(i, i + size) for i in range(0, width, size)]


def conv_rows(ext, taps, rows, cols):
    total = taps[0:1, :] * ext[HALO - 3 : HALO - 3 + rows, cols]
    for k in range(1, CONV):
        total = total + taps[k : k + 1, :] * ext[HALO - 3 + k : HALO - 3 + k + rows, cols]
    return total

MESH = pl.DeviceIdType.MESH
ROW_F = STATE + 8


def pair(ref, cols):
    first = cols.start // LANES
    return jnp.concatenate([ref[first], ref[first + 1]], axis=1)


def mixer_kernel(
    x_hbm, b_hbm, c_hbm, z_hbm, dtt_hbm, cx_hbm, cb_hbm, cc_hbm, bias_hbm, alog_hbm, dskip_hbm, gain_hbm, go_hbm,
    gx_hbm, gb_hbm, gc_hbm, dz_hbm, ddt_hbm, convx_hbm, convb_hbm, convc_hbm, bias_out, alog_out, skip_out, gain_out,
    x_in, bc_in, z_ref, dtt_ref, cx_ref, cbc_ref, bias_ref, alog_ref, dskip_ref, gain_ref, go_ref,
    halo_ref, extx, extbc, prex_ref, x_ref, prebc_ref, bc_ref, cumt_ref, dtx_ref, cumx_ref, skip_ref,
    y_ref, dy_ref, dxd_ref, inner, inner_grad,
    own_f, pair_f, chain_in_f, chain_out_f, back_f, enter_ref, own_b, pair_b, chain_in_b, chain_out_b, back_b, later_ref,
    own_p, slots_p, outs_p, total_p, taps_slots,
    sums_slots, early, slots_e, late, slots_l, final, taps_all, dpre_own, next_x, next_bc,
    gx_ref, gbc_ref, dz_ref, ddt_ref, convbc_ref, small_ref, bias_sum, alog_sum, skip_sum, gain_sum,
    load_sem, store_sem, ctx_send, ctx_recv, tp_send, tp_recv, halo_send, halo_recv,
):
    me, tp = lax.axis_index("ctx"), lax.axis_index("tp")
    count, lanes_of_heads = lax.axis_size("ctx"), lax.axis_size("tp")
    ranks = lanes_of_heads
    rows, width = x_in.shape
    half = GROUPS * STATE
    heads = dtt_ref.shape[0]
    parts = width // LANES
    stride = count // parts
    my_part = me // stride
    size = 2 * LANES

    loads = []

    def load(src, dst):
        copy = pltpu.make_async_copy(src, dst, load_sem.at[len(loads)])
        copy.start()
        loads.append(copy)

    load(x_hbm, x_in)
    load(b_hbm, bc_in.at[:, 0:half])
    load(c_hbm, bc_in.at[:, half:])
    load(dtt_hbm, dtt_ref)
    load(cx_hbm, cx_ref)
    load(cb_hbm, cbc_ref.at[:, 0:half])
    load(cc_hbm, cbc_ref.at[:, half:])
    load(bias_hbm, bias_ref)
    load(alog_hbm, alog_ref)
    load(dskip_hbm, dskip_ref)
    load(gain_hbm, gain_ref)
    load(z_hbm, z_ref)
    load(go_hbm, go_ref)

    barrier = pltpu.get_barrier_semaphore()
    for d in range(1, count):
        pl.semaphore_signal(barrier, inc=1, device_id=(lax.rem(me + d, count), tp), device_id_type=MESH)
    for d in range(1, ranks):
        pl.semaphore_signal(barrier, inc=1, device_id=(me, lax.rem(tp + d, ranks)), device_id_type=MESH)
    pl.semaphore_wait(barrier, count - 1 + ranks - 1)

    def remote(src, dst, send, recv, ctx, rank):
        return pltpu.make_async_remote_copy(
            src_ref=src, dst_ref=dst, send_sem=send, recv_sem=recv, device_id=(ctx, rank), device_id_type=MESH
        )

    ahead, behind = lax.rem(me + 1, count), lax.rem(me + count - 1, count)
    for copy in loads[0:3]:
        copy.wait()
    tail = [
        remote(x_in.at[rows - HALO :, :], halo_ref.at[:, 0:width], halo_send.at[0], halo_recv.at[0], ahead, tp),
        remote(bc_in.at[rows - HALO :, :], halo_ref.at[:, width:], halo_send.at[1], halo_recv.at[1], ahead, tp),
    ]

    @pl.when(me < count - 1)
    def _():
        for copy in tail:
            copy.start()

    for copy in loads[3:11]:
        copy.wait()

    step = jax.nn.softplus(jnp.transpose(dtt_ref[...]) + bias_ref[...])
    rate = jnp.exp(alog_ref[...])
    tril = (iota((rows, rows), 0) >= iota((rows, rows), 1)).astype(F32)
    cum = exact(tril, -rate * step)
    cumt_ref[...] = jnp.transpose(cum)
    spread = head_spread(heads, width)
    dtx_ref[...] = exact(step, spread)
    cumx_ref[...] = exact(cum, spread)
    skip_ref[...] = exact(jnp.broadcast_to(dskip_ref[...], (8, heads)), spread)
    extx[HALO:, :] = x_in[...].astype(F32)
    extbc[HALO:, :] = bc_in[...].astype(F32)

    @pl.when(me == 0)
    def _():
        extx[0:HALO, :] = jnp.zeros((HALO, width), F32)
        extbc[0:HALO, :] = jnp.zeros((HALO, 2 * half), F32)

    @pl.when(me > 0)
    def _():
        for copy in tail:
            copy.wait_recv()
        extx[0:HALO, :] = halo_ref[:, 0:width].astype(F32)
        extbc[0:HALO, :] = halo_ref[:, width:].astype(F32)

    for cols in tiles(2 * half, LANES):
        pre = conv_rows(extbc, cbc_ref[:, cols], rows, cols)
        prebc_ref[:, cols] = pre
        bc_ref[:, cols] = pre * sigmoid(pre)
    for cols in tiles(width, LANES):
        pre = conv_rows(extx, cx_ref[:, cols], rows, cols)
        prex_ref[:, cols] = pre
        x_ref[:, cols] = pre * sigmoid(pre)
    b_turned = split(jnp.transpose(bc_ref[:, 0:half]))
    for cols in tiles(width, size):
        cumx = cumx_ref[:, cols]
        end = cumx[rows - 1 : rows]
        weighted = jnp.exp(end - cumx) * dtx_ref[:, cols] * x_ref[:, cols]
        state = diagonal_blocks(mul(b_turned, split(weighted)))
        decay = jnp.broadcast_to(jnp.exp(end), (8, size))
        for i in range(2):
            own_f[cols.start // LANES + i, 0:STATE, :] = state[:, i * LANES : (i + 1) * LANES]
            own_f[cols.start // LANES + i, STATE:, :] = decay[:, i * LANES : (i + 1) * LANES]

    def to_owner(own, slots, k, part):
        return remote(own.at[part], slots.at[me], ctx_send.at[k, part], ctx_recv.at[k, me], part * stride, tp)

    def gather_tiles(own, slots, k):
        for d in range(1, parts):
            to_owner(own, slots, k, lax.rem(my_part + d, parts)).start()
        if stride > 1:
            @pl.when(lax.rem(me, stride) != 0)
            def _():
                to_owner(own, slots, k, my_part).start()

    def owner_only(act):
        if stride > 1:
            pl.when(lax.rem(me, stride) == 0)(act)
        else:
            act()

    def from_owner(out, result, k, i):
        return remote(out, result.at[my_part], ctx_send.at[k + 1, i], ctx_recv.at[k + 1, my_part], i, tp)

    def slot_wait(slots, k, j):
        @pl.when(j != me)
        def _():
            remote(slots.at[j], slots.at[j], ctx_send.at[k, 0], ctx_recv.at[k, j], ahead, tp).wait_recv()

    def settle_exchange(own, slots, outs, result, k):
        for j in range(parts):
            @pl.when(me != j * stride)
            def _():
                remote(result.at[j], result.at[j], ctx_send.at[k + 1, 0], ctx_recv.at[k + 1, j], ahead, tp).wait_recv()

    def drain(own, slots, outs, result, k):
        for j in range(parts):
            @pl.when(me != j * stride)
            def _():
                to_owner(own, slots, k, j).wait_send()

        def sent():
            for i in range(count):
                @pl.when(me != i)
                def _():
                    from_owner(outs.at[0], result, k, i).wait_send()

        owner_only(sent)

    side = lax.rem(me, 2)
    partner = me + 1 - 2 * side
    half_parts = parts // 2

    def to_partner(own, pair_in, row, k):
        return remote(
            own.at[(1 - side) * half_parts + k], pair_in.at[k], ctx_send.at[row, k], ctx_recv.at[row, k], partner, tp
        )

    def to_next(chain_out, chain_in, row, k, there):
        return remote(chain_out.at[k], chain_in.at[k], ctx_send.at[row + 2, k], ctx_recv.at[row + 2, k], there, tp)

    def hand_back(back, result, row, k, part):
        return remote(back.at[k], result.at[part], ctx_send.at[row + 1, k], ctx_recv.at[row + 1, k], partner, tp)

    def swap_halves(own, pair_in, row):
        for k in range(half_parts):
            to_partner(own, pair_in, row, k).start()

    def pair_scan(own, pair_in, chain_in, chain_out, back, result, row, backward, between):
        if backward:
            there, has_prev, has_next, leads = lax.rem(me + count - 2, count), me < count - 2, me >= 2, side == 1
        else:
            there, has_prev, has_next, leads = lax.rem(me + 2, count), me >= 2, me < count - 2, side == 0
        for k in range(half_parts):
            part = side * half_parts + k
            to_partner(own, pair_in, row, k).wait_recv()
            mine, other = own[part], pair_in[k]
            mine_decay, other_decay = own_f[part][STATE : STATE + 1], pair_f[k][STATE : STATE + 1]
            first = jnp.where(leads, mine[0:STATE], other[0:STATE])
            second = jnp.where(leads, other[0:STATE], mine[0:STATE])
            first_decay = jnp.where(leads, mine_decay, other_decay)
            second_decay = jnp.where(leads, other_decay, mine_decay)

            @pl.when(has_prev)
            def _():
                to_next(chain_out, chain_in, row, k, there).wait_recv()

            @pl.when(jnp.logical_not(has_prev))
            def _():
                chain_in[k] = jnp.zeros((STATE, LANES), F32)

            coming = chain_in[k]
            middle = first_decay * coming + first

            @pl.when(has_next)
            def _():
                chain_out[k] = second_decay * middle + second
                to_next(chain_out, chain_in, row, k, there).start()

            result[part] = jnp.where(leads, coming, middle)
            back[k] = jnp.where(leads, middle, coming)
            hand_back(back, result, row, k, part).start()
            between(k)

        def finish():
            for k in range(half_parts):
                hand_back(back, result, row, k, (1 - side) * half_parts + k).wait_recv()

        def drain_scan():
            for k in range(half_parts):
                to_partner(own, pair_in, row, k).wait_send()
                hand_back(back, result, row, k, side * half_parts + k).wait_send()

            @pl.when(has_next)
            def _():
                for k in range(half_parts):
                    to_next(chain_out, chain_in, row, k, there).wait_send()

        return finish, drain_scan

    swap_halves(own_f, pair_f, 0)

    owner = lane_group(LANES)
    causal = iota((rows, rows), 0) >= iota((rows, rows), 1)
    for g in range(GROUPS):
        c_g = split(bc_ref[:, half + g * STATE : half + (g + 1) * STATE])
        inner[g] = mul(c_g, split(bc_ref[:, g * STATE : (g + 1) * STATE]), MT)

    def inside(r):
        cols = slice(r * LANES, (r + 1) * LANES)
        x = x_ref[:, cols]
        weighted = x * dtx_ref[:, cols]
        cumx = cumx_ref[:, cols]
        total = skip_ref[0:1, cols] * x
        for g in range(GROUPS):
            h = r * GROUPS + g
            gap = cumx[:, g * HEAD_DIM : g * HEAD_DIM + 1] - cumt_ref[h : h + 1, :]
            fade = jnp.exp(jnp.where(causal, gap, -1e30)) * inner[g]
            total = total + mul(split(fade), split(jnp.where(owner == g, weighted, 0.0)))
        y_ref[:, cols] = total

    def two_inside(k):
        inside(2 * k)
        inside(2 * k + 1)

    finish_f, drain_f = pair_scan(
        own_f, pair_f, chain_in_f, chain_out_f, back_f, enter_ref, 0, False, two_inside
    )
    for copy in loads[11:]:
        copy.wait()
    finish_f()

    c_all = split(bc_ref[:, half:])
    squares = jnp.zeros((rows, LANES), F32)
    inners = jnp.zeros((rows, LANES), F32)
    for cols in tiles(width, size):
        carried = mul(c_all, split(block_diagonal(pair(enter_ref, cols))))
        y = y_ref[:, cols] + jnp.exp(cumx_ref[:, cols]) * carried
        y_ref[:, cols] = y
        z = z_ref[:, cols].astype(F32)
        gated = y * (z * sigmoid(z))
        scaled = go_ref[:, cols].astype(F32) * gain_ref[:, cols]
        sq = gated * gated
        pr = scaled * gated
        squares = squares + sq[:, :LANES] + sq[:, LANES:]
        inners = inners + pr[:, :LANES] + pr[:, LANES:]
    pick = iota((2 * GROUPS, LANES), 1) // HEAD_DIM
    row = iota((2 * GROUPS, LANES), 0)
    pick_low = (pick == row).astype(F32)
    pick_high = (pick + GROUPS == row).astype(F32)
    sums_slots[tp] = exact(pick_low, squares, MT) + exact(pick_high, inners, MT)

    def tp_copies(own_at, dst_at, k):
        return [
            remote(own_at(q), dst_at, tp_send.at[k, q], tp_recv.at[k, tp], me, q)
            for q in [lax.rem(tp + d, ranks) for d in range(1, ranks)]
        ]

    def tp_wait(slots, k):
        for d in range(1, ranks):
            q = lax.rem(tp + d, ranks)
            remote(slots.at[q], slots.at[q], tp_send.at[k, q], tp_recv.at[k, q], me, q).wait_recv()

    started = []

    def tp_start(own_at, dst_at, k):
        copies = tp_copies(own_at, dst_at, k)
        for copy in copies:
            copy.start()
        started.extend(copies)

    tp_start(lambda q: sums_slots.at[tp], sums_slots.at[tp], 0)
    tp_wait(sums_slots, 0)
    sums = sums_slots[0]
    for q in range(1, ranks):
        sums = sums + sums_slots[q]
    group_width = width * ranks // GROUPS
    turned = jnp.transpose(sums)
    inverse = lax.rsqrt(exact(turned, pick_low) / group_width + EPSILON)
    correction = inverse * inverse * inverse * exact(turned, pick_high) / group_width
    inverse = jnp.concatenate([inverse, inverse], axis=1)
    correction = jnp.concatenate([correction, correction], axis=1)
    c_turned = split(jnp.transpose(bc_ref[:, half:]))
    own_p[...] = jnp.zeros_like(own_p)
    for cols in tiles(width, size):
        y = y_ref[:, cols]
        z = z_ref[:, cols].astype(F32)
        s = sigmoid(z)
        gate = z * s
        gated = y * gate
        go = go_ref[:, cols].astype(F32)
        gain_grad = jnp.sum(go * gated * inverse, axis=0, keepdims=True)
        gated_grad = inverse * (go * gain_ref[:, cols]) - gated * correction
        dy = gated_grad * gate
        dy_ref[:, cols] = dy
        dz_ref[:, cols] = (gated_grad * y * (s * (1.0 + z * (1.0 - s)))).astype(BF16)
        state = diagonal_blocks(mul(c_turned, split(jnp.exp(cumx_ref[:, cols]) * dy)))
        for i in range(2):
            part = slice(i * LANES, (i + 1) * LANES)
            own_b[cols.start // LANES + i] = state[:, part]
            own_p[cols.start // LANES + i, 4:5, :] = gain_grad[:, part]
    swap_halves(own_b, pair_b, 3)

    stores = []

    def store(src, dst):
        copy = pltpu.make_async_copy(src, dst, store_sem.at[len(stores)])
        copy.start()
        stores.append(copy)

    store(dz_ref, dz_hbm)

    for g in range(GROUPS):
        c_g = split(bc_ref[:, half + g * STATE : half + (g + 1) * STATE])
        inner[g] = mul(split(bc_ref[:, g * STATE : (g + 1) * STATE]), c_g, MT)
    inner_grad[...] = jnp.zeros_like(inner_grad)
    causal_back = iota((rows, rows), 0) <= iota((rows, rows), 1)
    dc = jnp.zeros((rows, half), F32)
    for cols in tiles(width, size):
        pushed = jnp.exp(cumx_ref[:, cols]) * dy_ref[:, cols]
        dc = dc + mul(split(pushed), split(block_diagonal(pair(enter_ref, cols))), MT)
    for g in range(GROUPS):
        early[g, rows:, :] = dc[:, g * STATE : (g + 1) * STATE]

    def inside_back(r):
        cols = slice(r * LANES, (r + 1) * LANES)
        dy = dy_ref[:, cols]
        cumx = cumx_ref[:, cols]
        weighted = split(x_ref[:, cols] * dtx_ref[:, cols])
        total = jnp.zeros((rows, LANES), F32)
        for g in range(GROUPS):
            h = r * GROUPS + g
            gap = cumt_ref[h : h + 1, :] - cumx[:, g * HEAD_DIM : g * HEAD_DIM + 1]
            decay = jnp.exp(jnp.where(causal_back, gap, -1e30))
            masked = split(jnp.where(owner == g, dy, 0.0))
            total = total + mul(split(decay * inner[g]), masked)
            inner_grad[g] = inner_grad[g] + decay * mul(weighted, masked, MT)
        dxd_ref[:, cols] = total

    def two_inside_back(k):
        inside_back(2 * k)
        inside_back(2 * k + 1)

    finish_b, drain_b = pair_scan(
        own_b, pair_b, chain_in_b, chain_out_b, back_b, later_ref, 3, True, two_inside_back
    )
    for g in range(GROUPS):
        own = slice(g * STATE, (g + 1) * STATE)
        other = slice(half + g * STATE, half + (g + 1) * STATE)
        grad = inner_grad[g]
        early[g, 0:rows, :] = mul(split(grad), split(bc_ref[:, other]))
        early[g, rows:, :] = early[g, rows:, :] + mul(split(jnp.transpose(grad)), split(bc_ref[:, own]))
    tp_start(lambda q: early.at[q], slots_e.at[tp], 1)

    finish_b()

    db = jnp.zeros((rows, half), F32)
    for cols in tiles(width, size):
        wide = split(block_diagonal(pair(later_ref, cols)))
        cumx = cumx_ref[:, cols]
        fade = jnp.exp(cumx[rows - 1 : rows] - cumx)
        db = db + mul(split(fade * (x_ref[:, cols] * dtx_ref[:, cols])), wide, MT)
    for g in range(GROUPS):
        late[g] = db[:, g * STATE : (g + 1) * STATE]
    tp_start(lambda q: late.at[q], slots_l.at[tp], 2)

    b_all = split(bc_ref[:, 0:half])
    cum_grad = jnp.zeros((rows, heads), F32)
    step_grad = jnp.zeros((rows, heads), F32)
    ends = jnp.zeros((8, heads), F32)
    skips = jnp.zeros((8, heads), F32)
    for cols in tiles(width, size):
        later = pair(later_ref, cols)
        cumx = cumx_ref[:, cols]
        end = cumx[rows - 1 : rows]
        x = x_ref[:, cols]
        dtx = dtx_ref[:, cols]
        dy = dy_ref[:, cols]
        weighted = x * dtx
        from_state = jnp.exp(end - cumx) * mul(b_all, split(block_diagonal(later)))
        dxd = dxd_ref[:, cols] + from_state
        skip = skip_ref[0:1, cols]
        dx = dtx * dxd + skip * dy
        spread = ((iota((heads, size), 1) + cols.start) // HEAD_DIM == iota((heads, size), 0)).astype(F32)
        cum_grad = cum_grad + exact(dy * (y_ref[:, cols] - skip * x) - weighted * dxd, spread, MT)
        step_grad = step_grad + exact(x * dxd, spread, MT)
        end_cols = jnp.sum(weighted * from_state, axis=0, keepdims=True) + jnp.exp(end) * jnp.sum(
            later * pair(enter_ref, cols), axis=0, keepdims=True
        )
        ends = ends + exact(jnp.broadcast_to(end_cols, (8, size)), spread, MT)
        skip_cols = jnp.sum(dy * x, axis=0, keepdims=True)
        skips = skips + exact(jnp.broadcast_to(skip_cols, (8, size)), spread, MT)
        dpre = dx * silu_slope(prex_ref[:, cols])
        dxd_ref[:, cols] = dpre
        for k in range(CONV):
            tap = jnp.sum(dpre * extx[HALO - 3 + k : HALO - 3 + k + rows, cols], axis=0, keepdims=True)
            for i in range(2):
                own_p[cols.start // LANES + i, k : k + 1, :] = tap[:, i * LANES : (i + 1) * LANES]
    send_x = remote(dxd_ref.at[0:8, :], next_x, halo_send.at[2], halo_recv.at[2], behind, tp)

    @pl.when(me > 0)
    def _():
        send_x.start()

    triu = (iota((rows, rows), 0) <= iota((rows, rows), 1)).astype(F32)
    log_grad = exact(triu, cum_grad) + ends[0:1]
    raw_grad = (step_grad - rate * log_grad) * sigmoid(jnp.transpose(dtt_ref[...]) + bias_ref[...])
    ddt_ref[...] = jnp.transpose(raw_grad)
    store(ddt_ref, ddt_hbm)
    small = [
        jnp.sum(raw_grad, axis=0, keepdims=True),
        jnp.sum(-rate * log_grad * step, axis=0, keepdims=True),
        skips[0:1],
    ]
    for i in range(3):
        own_p[i, 5:6, 0:heads] = small[i]

    gather_tiles(own_p, slots_p, 6)
    tp_wait(slots_e, 1)
    tp_wait(slots_l, 2)
    slots_e[tp] = early[tp]
    slots_l[tp] = late[tp]
    both = slots_e[0]
    db = slots_l[0]
    for q in range(1, ranks):
        both = both + slots_e[q]
        db = db + slots_l[q]
    for i, grad in ((0, both[0:rows] + db), (1, both[rows:])):
        mine = pl.ds(pl.multiple_of(i * half + tp * LANES, LANES), LANES)
        dpre = grad * silu_slope(prebc_ref[:, mine])
        dpre_own[i, 0:rows, :] = dpre
        for k in range(CONV):
            taps_slots[me, i * CONV + k : i * CONV + k + 1, :] = jnp.sum(
                dpre * extbc[HALO - 3 + k : HALO - 3 + k + rows, mine], axis=0, keepdims=True
            )
    send_bc = remote(dpre_own.at[:, 0:8, :], next_bc, halo_send.at[3], halo_recv.at[3], behind, tp)

    @pl.when(me > 0)
    def _():
        send_bc.start()

    def to_all(i):
        return remote(taps_slots.at[me], taps_slots.at[me], ctx_send.at[8, i], ctx_recv.at[8, me], i, tp)

    for d in range(1, count):
        to_all(lax.rem(me + d, count)).start()

    extx[0:rows, :] = dxd_ref[...]

    @pl.when(me < count - 1)
    def _():
        send_x.wait_recv()
        extx[rows : rows + 8, :] = next_x[...]

    @pl.when(me == count - 1)
    def _():
        extx[rows : rows + 8, :] = jnp.zeros((8, width), F32)

    for cols in tiles(width, LANES):
        total = cx_ref[0:1, cols] * extx[3 : 3 + rows, cols]
        for k in range(1, CONV):
            total = total + cx_ref[k : k + 1, cols] * extx[3 - k : 3 - k + rows, cols]
        gx_ref[:, cols] = total.astype(BF16)
    store(gx_ref, gx_hbm)

    def sum_parts():
        slots_p[me] = own_p[my_part]
        for j in range(count):
            slot_wait(slots_p, 6, j)
        total = slots_p[0]
        for j in range(1, count):
            total = total + slots_p[j]
        outs_p[0] = total
        for d in range(1, count):
            from_owner(outs_p.at[0], total_p, 6, lax.rem(me + d, count)).start()
        total_p[my_part] = total

    owner_only(sum_parts)

    @pl.when(me < count - 1)
    def _():
        send_bc.wait_recv()
        dpre_own[:, rows : rows + 8, :] = next_bc[...]

    @pl.when(me == count - 1)
    def _():
        dpre_own[:, rows : rows + 8, :] = jnp.zeros((2, 8, LANES), F32)

    for i in range(2):
        taps = cbc_ref[:, pl.ds(pl.multiple_of(i * half + tp * LANES, LANES), LANES)]
        total = taps[0:1] * dpre_own[i, 3 : 3 + rows, :]
        for k in range(1, CONV):
            total = total + taps[k : k + 1] * dpre_own[i, 3 - k : 3 - k + rows, :]
        final[tp, i * rows : (i + 1) * rows, :] = total.astype(BF16)
    tp_start(lambda q: final.at[tp], final.at[tp], 3)

    for j in range(count):
        slot_wait(taps_slots, 8, j)
    taps_sum = taps_slots[0]
    for j in range(1, count):
        taps_sum = taps_sum + taps_slots[j]
    taps_all[tp] = taps_sum
    tp_start(lambda q: taps_all.at[tp], taps_all.at[tp], 4)

    settle_exchange(own_p, slots_p, outs_p, total_p, 6)
    for r, cols in enumerate(tiles(width, LANES)):
        small_ref[:, cols] = total_p[r, 0:CONV, :]
        gain_sum[:, cols] = total_p[r, 4:5, :]
    bias_sum[...] = total_p[0, 5:6, 0:heads]
    alog_sum[...] = total_p[1, 5:6, 0:heads]
    skip_sum[...] = total_p[2, 5:6, 0:heads]
    store(small_ref, convx_hbm)
    store(gain_sum, gain_out)
    store(bias_sum, bias_out)
    store(alog_sum, alog_out)
    store(skip_sum, skip_out)

    tp_wait(final, 3)
    for q in range(ranks):
        for i in range(2):
            gbc_ref[i, :, q * STATE : (q + 1) * STATE] = final[q, i * rows : (i + 1) * rows, :]
    store(gbc_ref.at[0], gb_hbm)
    store(gbc_ref.at[1], gc_hbm)
    tp_wait(taps_all, 4)
    for q in range(ranks):
        for i in range(2):
            convbc_ref[i, :, q * STATE : (q + 1) * STATE] = taps_all[q, i * CONV : (i + 1) * CONV, :]
    store(convbc_ref.at[0], convb_hbm)
    store(convbc_ref.at[1], convc_hbm)

    @pl.when(me < count - 1)
    def _():
        for copy in tail:
            copy.wait_send()

    @pl.when(me > 0)
    def _():
        send_x.wait_send()
        send_bc.wait_send()

    drain_f()
    drain_b()
    drain(own_p, slots_p, outs_p, total_p, 6)
    for d in range(1, count):
        to_all(lax.rem(me + d, count)).wait_send()
    for copy in started:
        copy.wait_send()
    for copy in stores:
        copy.wait()


def deliver_kernel(*refs):
    number = len(refs) // 2
    sem = refs[-1]
    copies = [pltpu.make_async_copy(refs[i], refs[number + i], sem.at[i]) for i in range(number)]
    for copy in copies:
        copy.start()
    for copy in copies:
        copy.wait()


def body(
    x_raw, b_raw, c_raw, z_gate, dt_raw, conv_x, conv_b, conv_c, dt_bias, a_log, d_skip, gain, grad_out
):
    rows, width = x_raw.shape
    heads = dt_raw.shape[1]
    half = b_raw.shape[1]
    count, ranks = lax.axis_size("ctx"), lax.axis_size("tp")
    parts = width // LANES
    hbm = pl.BlockSpec(memory_space=pl.ANY)

    def f32(*shape):
        return pltpu.VMEM(shape, F32)

    def b16(*shape):
        return pltpu.VMEM(shape, BF16)

    full, shared = f32(rows, width), f32(rows, 2 * half)
    outs = [
        ((rows, width), BF16), ((rows, half), BF16), ((rows, half), BF16), ((rows, width), BF16), ((heads, rows), F32),
        ((CONV, width), F32), ((CONV, half), F32), ((CONV, half), F32), ((1, heads), F32), ((1, heads), F32),
        ((1, heads), F32), ((1, width), F32),
    ]
    scratch = [
        b16(rows, width), b16(rows, 2 * half), b16(rows, width), f32(heads, rows), f32(CONV, width),
        f32(CONV, 2 * half), f32(1, heads), f32(1, heads), f32(1, heads), f32(1, width), b16(rows, width),
        b16(HALO, width + 2 * half), f32(HALO + rows, width), f32(HALO + rows, 2 * half), full, full, shared, shared,
        f32(heads, rows), full, full, f32(8, width),
        full, full, full, f32(GROUPS, rows, rows), f32(GROUPS, rows, rows),
        f32(parts, ROW_F, LANES), f32(parts // 2, ROW_F, LANES), *[f32(parts // 2, STATE, LANES)] * 3,
        f32(parts, STATE, LANES),
        f32(parts, STATE, LANES), *[f32(parts // 2, STATE, LANES)] * 4, f32(parts, STATE, LANES),
        f32(parts, 8, LANES), f32(count, 8, LANES), f32(1, 8, LANES), f32(parts, 8, LANES), f32(count, 8, LANES),
        f32(ranks, 8, rows), f32(ranks, 2 * rows, LANES), f32(ranks, 2 * rows, LANES), f32(ranks, rows, LANES),
        f32(ranks, rows, LANES), b16(ranks, 2 * rows, LANES), f32(ranks, 8, LANES), f32(2, rows + 8, LANES),
        f32(8, width), f32(2, 8, LANES),
        b16(rows, width), b16(2, rows, half), b16(rows, width), f32(heads, rows), f32(2, CONV, half), f32(CONV, width),
        f32(1, heads), f32(1, heads), f32(1, heads), f32(1, width),
    ] + [
        pltpu.SemaphoreType.DMA(s)
        for s in ((13,), (12,), (9, count), (9, count), (5, ranks), (5, ranks), (4,), (4,))
    ]
    shapes = [jax.ShapeDtypeStruct(s, d) for s, d in outs]
    results = pl.pallas_call(
        mixer_kernel,
        out_shape=shapes,
        in_specs=[hbm] * 13,
        out_specs=[hbm] * len(outs),
        scratch_shapes=scratch,
        compiler_params=pltpu.CompilerParams(
            collective_id=0, has_side_effects=True, vmem_limit_bytes=56 * 1024 * 1024
        ),
    )(
        x_raw, b_raw, c_raw, z_gate, dt_raw.T, conv_x, conv_b, conv_c, dt_bias[None], a_log[None], d_skip[None],
        gain[None], grad_out,
    )
    gx, gb, gc, dz, ddt, convx, convb, convc, bias, alog, skip, gain_grad = pl.pallas_call(
        deliver_kernel,
        out_shape=shapes,
        in_specs=[hbm] * len(outs),
        out_specs=[hbm] * len(outs),
        scratch_shapes=[pltpu.SemaphoreType.DMA((len(outs),))],
        compiler_params=pltpu.CompilerParams(vmem_limit_bytes=56 * 1024 * 1024),
    )(*results)
    return gx, gb, gc, dz, ddt.T, convx, convb, convc, bias[0], alog[0], skip[0], gain_grad[0]


def solution(mesh):
    col, row, cut = P("ctx", "tp"), P("ctx", None), P("tp")
    return jax.shard_map(
        body,
        mesh=mesh,
        in_specs=(col, row, row, col, col, P(None, "tp"), P(), P(), cut, cut, cut, cut, col),
        out_specs=(col, row, row, col, col, P(None, "tp"), P(), P(), cut, cut, cut, cut),
        check_vma=False,
    )
```

```python
import functools

import jax
import jax.numpy as jnp
from jax import lax
from jax.experimental import pallas as pl
from jax.experimental.pallas import tpu as pltpu
from jax.sharding import PartitionSpec as P

HEAD_DIM = 32
STATE = 128
GROUPS = 4
CONV = 4
HALO = 16
LANES = 128
EPSILON = 1e-05
F32 = jnp.float32
BF16 = jnp.bfloat16
MM = ((1,), (0,))
MT = ((1,), (1,))


def split(value):
    high = value.astype(BF16)
    return high, (value - high.astype(F32)).astype(BF16)


def mul(a, b, dims=MM):
    def dot(u, v):
        return lax.dot_general(u, v, (dims, ((), ())), preferred_element_type=F32)

    return dot(a[0], b[0]) + (dot(a[0], b[1]) + dot(a[1], b[0]))


def exact(a, b, dims=MM):
    return lax.dot_general(
        a, b, (dims, ((), ())), preferred_element_type=F32, precision=lax.Precision.HIGHEST
    )


def sigmoid(v):
    return 1.0 / (1.0 + jnp.exp(-v))


def silu_slope(v):
    s = sigmoid(v)
    return s * (1.0 + v * (1.0 - s))


def iota(shape, axis):
    return lax.broadcasted_iota(jnp.int32, shape, axis)


def lane_group(width):
    return (iota((1, width), 1) // HEAD_DIM) % GROUPS


def head_spread(heads, width):
    return (iota((heads, width), 1) // HEAD_DIM == iota((heads, width), 0)).astype(F32)


def block_diagonal(state):
    owner = lane_group(state.shape[1])
    return jnp.concatenate([jnp.where(owner == g, state, 0.0) for g in range(GROUPS)], axis=0)


def diagonal_blocks(stacked):
    owner = lane_group(stacked.shape[1])
    total = jnp.zeros((STATE, stacked.shape[1]), F32)
    for g in range(GROUPS):
        total = jnp.where(owner == g, stacked[g * STATE : (g + 1) * STATE], total)
    return total


def tiles(width, size):
    return [slice(i, i + size) for i in range(0, width, size)]


def conv_rows(ext, taps, rows, cols):
    total = taps[0:1, :] * ext[HALO - 3 : HALO - 3 + rows, cols]
    for k in range(1, CONV):
        total = total + taps[k : k + 1, :] * ext[HALO - 3 + k : HALO - 3 + k + rows, cols]
    return total

MESH = pl.DeviceIdType.MESH
ROW_F = STATE + 8


def pair(ref, cols):
    first = cols.start // LANES
    return jnp.concatenate([ref[first], ref[first + 1]], axis=1)


def mixer_kernel(
    x_hbm, b_hbm, c_hbm, z_hbm, dtt_hbm, cx_hbm, cb_hbm, cc_hbm, bias_hbm, alog_hbm, dskip_hbm, gain_hbm, go_hbm,
    gx_hbm, gb_hbm, gc_hbm, dz_hbm, ddt_hbm, convx_hbm, convb_hbm, convc_hbm, bias_out, alog_out, skip_out, gain_out,
    x_in, bc_in, z_ref, dtt_ref, cx_ref, cbc_ref, bias_ref, alog_ref, dskip_ref, gain_ref, go_ref,
    halo_ref, extx, extbc, prex_ref, x_ref, prebc_ref, bc_ref, cumt_ref, dtx_ref, cumx_ref, skip_ref,
    y_ref, dy_ref, dxd_ref, inner, inner_grad,
    own_f, pair_f, chain_in_f, chain_out_f, back_f, enter_ref, own_b, pair_b, chain_in_b, chain_out_b, back_b, later_ref,
    own_p, slots_p, outs_p, total_p, taps_slots,
    sums_slots, early, slots_e, late, slots_l, final, taps_all, dpre_own, next_x, next_bc,
    gx_ref, gbc_ref, dz_ref, ddt_ref, convbc_ref, small_ref, bias_sum, alog_sum, skip_sum, gain_sum,
    load_sem, store_sem, ctx_send, ctx_recv, tp_send, tp_recv, halo_send, halo_recv,
):
    me, tp = lax.axis_index("ctx"), lax.axis_index("tp")
    count, lanes_of_heads = lax.axis_size("ctx"), lax.axis_size("tp")
    ranks = lanes_of_heads
    rows, width = x_in.shape
    half = GROUPS * STATE
    heads = dtt_ref.shape[0]
    parts = width // LANES
    stride = count // parts
    my_part = me // stride
    size = 2 * LANES

    loads = []

    def load(src, dst):
        copy = pltpu.make_async_copy(src, dst, load_sem.at[len(loads)])
        copy.start()
        loads.append(copy)

    load(x_hbm, x_in)
    load(b_hbm, bc_in.at[:, 0:half])
    load(c_hbm, bc_in.at[:, half:])
    load(dtt_hbm, dtt_ref)
    load(cx_hbm, cx_ref)
    load(cb_hbm, cbc_ref.at[:, 0:half])
    load(cc_hbm, cbc_ref.at[:, half:])
    load(bias_hbm, bias_ref)
    load(alog_hbm, alog_ref)
    load(dskip_hbm, dskip_ref)
    load(gain_hbm, gain_ref)
    load(z_hbm, z_ref)
    load(go_hbm, go_ref)

    barrier = pltpu.get_barrier_semaphore()
    for d in range(1, count):
        pl.semaphore_signal(barrier, inc=1, device_id=(lax.rem(me + d, count), tp), device_id_type=MESH)
    for d in range(1, ranks):
        pl.semaphore_signal(barrier, inc=1, device_id=(me, lax.rem(tp + d, ranks)), device_id_type=MESH)
    pl.semaphore_wait(barrier, count - 1 + ranks - 1)

    def remote(src, dst, send, recv, ctx, rank):
        return pltpu.make_async_remote_copy(
            src_ref=src, dst_ref=dst, send_sem=send, recv_sem=recv, device_id=(ctx, rank), device_id_type=MESH
        )

    ahead, behind = lax.rem(me + 1, count), lax.rem(me + count - 1, count)
    for copy in loads[0:3]:
        copy.wait()
    tail = [
        remote(x_in.at[rows - HALO :, :], halo_ref.at[:, 0:width], halo_send.at[0], halo_recv.at[0], ahead, tp),
        remote(bc_in.at[rows - HALO :, :], halo_ref.at[:, width:], halo_send.at[1], halo_recv.at[1], ahead, tp),
    ]

    @pl.when(me < count - 1)
    def _():
        for copy in tail:
            copy.start()

    for copy in loads[3:11]:
        copy.wait()

    step = jax.nn.softplus(jnp.transpose(dtt_ref[...]) + bias_ref[...])
    rate = jnp.exp(alog_ref[...])
    tril = (iota((rows, rows), 0) >= iota((rows, rows), 1)).astype(F32)
    cum = exact(tril, -rate * step)
    cumt_ref[...] = jnp.transpose(cum)
    spread = head_spread(heads, width)
    dtx_ref[...] = exact(step, spread)
    cumx_ref[...] = exact(cum, spread)
    skip_ref[...] = exact(jnp.broadcast_to(dskip_ref[...], (8, heads)), spread)
    extx[HALO:, :] = x_in[...].astype(F32)
    extbc[HALO:, :] = bc_in[...].astype(F32)

    @pl.when(me == 0)
    def _():
        extx[0:HALO, :] = jnp.zeros((HALO, width), F32)
        extbc[0:HALO, :] = jnp.zeros((HALO, 2 * half), F32)

    @pl.when(me > 0)
    def _():
        for copy in tail:
            copy.wait_recv()
        extx[0:HALO, :] = halo_ref[:, 0:width].astype(F32)
        extbc[0:HALO, :] = halo_ref[:, width:].astype(F32)

    for cols in tiles(2 * half, LANES):
        pre = conv_rows(extbc, cbc_ref[:, cols], rows, cols)
        prebc_ref[:, cols] = pre
        bc_ref[:, cols] = pre * sigmoid(pre)
    for cols in tiles(width, LANES):
        pre = conv_rows(extx, cx_ref[:, cols], rows, cols)
        prex_ref[:, cols] = pre
        x_ref[:, cols] = pre * sigmoid(pre)
    b_turned = split(jnp.transpose(bc_ref[:, 0:half]))
    for cols in tiles(width, size):
        cumx = cumx_ref[:, cols]
        end = cumx[rows - 1 : rows]
        weighted = jnp.exp(end - cumx) * dtx_ref[:, cols] * x_ref[:, cols]
        state = diagonal_blocks(mul(b_turned, split(weighted)))
        decay = jnp.broadcast_to(jnp.exp(end), (8, size))
        for i in range(2):
            own_f[cols.start // LANES + i, 0:STATE, :] = state[:, i * LANES : (i + 1) * LANES]
            own_f[cols.start // LANES + i, STATE:, :] = decay[:, i * LANES : (i + 1) * LANES]

    def to_owner(own, slots, k, part):
        return remote(own.at[part], slots.at[me], ctx_send.at[k, part], ctx_recv.at[k, me], part * stride, tp)

    def gather_tiles(own, slots, k):
        for d in range(1, parts):
            to_owner(own, slots, k, lax.rem(my_part + d, parts)).start()
        if stride > 1:
            @pl.when(lax.rem(me, stride) != 0)
            def _():
                to_owner(own, slots, k, my_part).start()

    def owner_only(act):
        if stride > 1:
            pl.when(lax.rem(me, stride) == 0)(act)
        else:
            act()

    def from_owner(out, result, k, i):
        return remote(out, result.at[my_part], ctx_send.at[k + 1, i], ctx_recv.at[k + 1, my_part], i, tp)

    def slot_wait(slots, k, j):
        @pl.when(j != me)
        def _():
            remote(slots.at[j], slots.at[j], ctx_send.at[k, 0], ctx_recv.at[k, j], ahead, tp).wait_recv()

    def settle_exchange(own, slots, outs, result, k):
        for j in range(parts):
            @pl.when(me != j * stride)
            def _():
                remote(result.at[j], result.at[j], ctx_send.at[k + 1, 0], ctx_recv.at[k + 1, j], ahead, tp).wait_recv()

    def drain(own, slots, outs, result, k):
        for j in range(parts):
            @pl.when(me != j * stride)
            def _():
                to_owner(own, slots, k, j).wait_send()

        def sent():
            for i in range(count):
                @pl.when(me != i)
                def _():
                    from_owner(outs.at[0], result, k, i).wait_send()

        owner_only(sent)

    side = lax.rem(me, 2)
    partner = me + 1 - 2 * side
    half_parts = parts // 2

    def to_partner(own, pair_in, row, k):
        return remote(
            own.at[(1 - side) * half_parts + k], pair_in.at[k], ctx_send.at[row, k], ctx_recv.at[row, k], partner, tp
        )

    def to_next(chain_out, chain_in, row, k, there):
        return remote(chain_out.at[k], chain_in.at[k], ctx_send.at[row + 2, k], ctx_recv.at[row + 2, k], there, tp)

    def hand_back(back, result, row, k, part):
        return remote(back.at[k], result.at[part], ctx_send.at[row + 1, k], ctx_recv.at[row + 1, k], partner, tp)

    def swap_halves(own, pair_in, row):
        for k in range(half_parts):
            to_partner(own, pair_in, row, k).start()

    def pair_scan(own, pair_in, chain_in, chain_out, back, result, row, backward, between):
        if backward:
            there, has_prev, has_next, leads = lax.rem(me + count - 2, count), me < count - 2, me >= 2, side == 1
        else:
            there, has_prev, has_next, leads = lax.rem(me + 2, count), me >= 2, me < count - 2, side == 0
        for k in range(half_parts):
            part = side * half_parts + k
            to_partner(own, pair_in, row, k).wait_recv()
            mine, other = own[part], pair_in[k]
            mine_decay, other_decay = own_f[part][STATE : STATE + 1], pair_f[k][STATE : STATE + 1]
            first = jnp.where(leads, mine[0:STATE], other[0:STATE])
            second = jnp.where(leads, other[0:STATE], mine[0:STATE])
            first_decay = jnp.where(leads, mine_decay, other_decay)
            second_decay = jnp.where(leads, other_decay, mine_decay)

            @pl.when(has_prev)
            def _():
                to_next(chain_out, chain_in, row, k, there).wait_recv()

            @pl.when(jnp.logical_not(has_prev))
            def _():
                chain_in[k] = jnp.zeros((STATE, LANES), F32)

            coming = chain_in[k]
            middle = first_decay * coming + first

            @pl.when(has_next)
            def _():
                chain_out[k] = second_decay * middle + second
                to_next(chain_out, chain_in, row, k, there).start()

            result[part] = jnp.where(leads, coming, middle)
            back[k] = jnp.where(leads, middle, coming)
            hand_back(back, result, row, k, part).start()
            between(k)

        def finish():
            for k in range(half_parts):
                hand_back(back, result, row, k, (1 - side) * half_parts + k).wait_recv()

        def drain_scan():
            for k in range(half_parts):
                to_partner(own, pair_in, row, k).wait_send()
                hand_back(back, result, row, k, side * half_parts + k).wait_send()

            @pl.when(has_next)
            def _():
                for k in range(half_parts):
                    to_next(chain_out, chain_in, row, k, there).wait_send()

        return finish, drain_scan

    swap_halves(own_f, pair_f, 0)

    owner = lane_group(LANES)
    causal = iota((rows, rows), 0) >= iota((rows, rows), 1)
    for g in range(GROUPS):
        c_g = split(bc_ref[:, half + g * STATE : half + (g + 1) * STATE])
        inner[g] = mul(c_g, split(bc_ref[:, g * STATE : (g + 1) * STATE]), MT)

    def inside(r):
        cols = slice(r * LANES, (r + 1) * LANES)
        x = x_ref[:, cols]
        weighted = x * dtx_ref[:, cols]
        cumx = cumx_ref[:, cols]
        total = skip_ref[0:1, cols] * x
        for g in range(GROUPS):
            h = r * GROUPS + g
            gap = cumx[:, g * HEAD_DIM : g * HEAD_DIM + 1] - cumt_ref[h : h + 1, :]
            fade = jnp.exp(jnp.where(causal, gap, -1e30)) * inner[g]
            total = total + mul(split(fade), split(jnp.where(owner == g, weighted, 0.0)))
        y_ref[:, cols] = total

    def two_inside(k):
        inside(2 * k)
        inside(2 * k + 1)

    finish_f, drain_f = pair_scan(
        own_f, pair_f, chain_in_f, chain_out_f, back_f, enter_ref, 0, False, two_inside
    )
    for copy in loads[11:]:
        copy.wait()
    finish_f()

    c_all = split(bc_ref[:, half:])
    squares = jnp.zeros((rows, LANES), F32)
    inners = jnp.zeros((rows, LANES), F32)
    for cols in tiles(width, size):
        carried = mul(c_all, split(block_diagonal(pair(enter_ref, cols))))
        y = y_ref[:, cols] + jnp.exp(cumx_ref[:, cols]) * carried
        y_ref[:, cols] = y
        z = z_ref[:, cols].astype(F32)
        gated = y * (z * sigmoid(z))
        scaled = go_ref[:, cols].astype(F32) * gain_ref[:, cols]
        sq = gated * gated
        pr = scaled * gated
        squares = squares + sq[:, :LANES] + sq[:, LANES:]
        inners = inners + pr[:, :LANES] + pr[:, LANES:]
    pick = iota((2 * GROUPS, LANES), 1) // HEAD_DIM
    row = iota((2 * GROUPS, LANES), 0)
    pick_low = (pick == row).astype(F32)
    pick_high = (pick + GROUPS == row).astype(F32)
    sums_slots[tp] = exact(pick_low, squares, MT) + exact(pick_high, inners, MT)

    def tp_copies(own_at, dst_at, k):
        return [
            remote(own_at(q), dst_at, tp_send.at[k, q], tp_recv.at[k, tp], me, q)
            for q in [lax.rem(tp + d, ranks) for d in range(1, ranks)]
        ]

    def tp_wait(slots, k):
        for d in range(1, ranks):
            q = lax.rem(tp + d, ranks)
            remote(slots.at[q], slots.at[q], tp_send.at[k, q], tp_recv.at[k, q], me, q).wait_recv()

    started = []

    def tp_start(own_at, dst_at, k):
        copies = tp_copies(own_at, dst_at, k)
        for copy in copies:
            copy.start()
        started.extend(copies)

    tp_start(lambda q: sums_slots.at[tp], sums_slots.at[tp], 0)
    tp_wait(sums_slots, 0)
    sums = sums_slots[0]
    for q in range(1, ranks):
        sums = sums + sums_slots[q]
    group_width = width * ranks // GROUPS
    turned = jnp.transpose(sums)
    inverse = lax.rsqrt(exact(turned, pick_low) / group_width + EPSILON)
    correction = inverse * inverse * inverse * exact(turned, pick_high) / group_width
    inverse = jnp.concatenate([inverse, inverse], axis=1)
    correction = jnp.concatenate([correction, correction], axis=1)
    c_turned = split(jnp.transpose(bc_ref[:, half:]))
    own_p[...] = jnp.zeros_like(own_p)
    for cols in tiles(width, size):
        y = y_ref[:, cols]
        z = z_ref[:, cols].astype(F32)
        s = sigmoid(z)
        gate = z * s
        gated = y * gate
        go = go_ref[:, cols].astype(F32)
        gain_grad = jnp.sum(go * gated * inverse, axis=0, keepdims=True)
        gated_grad = inverse * (go * gain_ref[:, cols]) - gated * correction
        dy = gated_grad * gate
        dy_ref[:, cols] = dy
        dz_ref[:, cols] = (gated_grad * y * (s * (1.0 + z * (1.0 - s)))).astype(BF16)
        state = diagonal_blocks(mul(c_turned, split(jnp.exp(cumx_ref[:, cols]) * dy)))
        for i in range(2):
            part = slice(i * LANES, (i + 1) * LANES)
            own_b[cols.start // LANES + i] = state[:, part]
            own_p[cols.start // LANES + i, 4:5, :] = gain_grad[:, part]
    swap_halves(own_b, pair_b, 3)

    stores = []

    def store(src, dst):
        copy = pltpu.make_async_copy(src, dst, store_sem.at[len(stores)])
        copy.start()
        stores.append(copy)

    store(dz_ref, dz_hbm)

    for g in range(GROUPS):
        c_g = split(bc_ref[:, half + g * STATE : half + (g + 1) * STATE])
        inner[g] = mul(split(bc_ref[:, g * STATE : (g + 1) * STATE]), c_g, MT)
    inner_grad[...] = jnp.zeros_like(inner_grad)
    causal_back = iota((rows, rows), 0) <= iota((rows, rows), 1)
    dc = jnp.zeros((rows, half), F32)
    for cols in tiles(width, size):
        pushed = jnp.exp(cumx_ref[:, cols]) * dy_ref[:, cols]
        dc = dc + mul(split(pushed), split(block_diagonal(pair(enter_ref, cols))), MT)
    for g in range(GROUPS):
        early[g, rows:, :] = dc[:, g * STATE : (g + 1) * STATE]

    def inside_back(r):
        cols = slice(r * LANES, (r + 1) * LANES)
        dy = dy_ref[:, cols]
        cumx = cumx_ref[:, cols]
        weighted = split(x_ref[:, cols] * dtx_ref[:, cols])
        total = jnp.zeros((rows, LANES), F32)
        for g in range(GROUPS):
            h = r * GROUPS + g
            gap = cumt_ref[h : h + 1, :] - cumx[:, g * HEAD_DIM : g * HEAD_DIM + 1]
            decay = jnp.exp(jnp.where(causal_back, gap, -1e30))
            masked = split(jnp.where(owner == g, dy, 0.0))
            total = total + mul(split(decay * inner[g]), masked)
            inner_grad[g] = inner_grad[g] + decay * mul(weighted, masked, MT)
        dxd_ref[:, cols] = total

    def two_inside_back(k):
        inside_back(2 * k)
        inside_back(2 * k + 1)

    finish_b, drain_b = pair_scan(
        own_b, pair_b, chain_in_b, chain_out_b, back_b, later_ref, 3, True, two_inside_back
    )
    for g in range(GROUPS):
        own = slice(g * STATE, (g + 1) * STATE)
        other = slice(half + g * STATE, half + (g + 1) * STATE)
        grad = inner_grad[g]
        early[g, 0:rows, :] = mul(split(grad), split(bc_ref[:, other]))
        early[g, rows:, :] = early[g, rows:, :] + mul(split(jnp.transpose(grad)), split(bc_ref[:, own]))
    tp_start(lambda q: early.at[q], slots_e.at[tp], 1)

    finish_b()

    db = jnp.zeros((rows, half), F32)
    for cols in tiles(width, size):
        wide = split(block_diagonal(pair(later_ref, cols)))
        cumx = cumx_ref[:, cols]
        fade = jnp.exp(cumx[rows - 1 : rows] - cumx)
        db = db + mul(split(fade * (x_ref[:, cols] * dtx_ref[:, cols])), wide, MT)
    for g in range(GROUPS):
        late[g] = db[:, g * STATE : (g + 1) * STATE]
    tp_start(lambda q: late.at[q], slots_l.at[tp], 2)

    b_all = split(bc_ref[:, 0:half])
    cum_grad = jnp.zeros((rows, heads), F32)
    step_grad = jnp.zeros((rows, heads), F32)
    ends = jnp.zeros((8, heads), F32)
    skips = jnp.zeros((8, heads), F32)
    for cols in tiles(width, size):
        later = pair(later_ref, cols)
        cumx = cumx_ref[:, cols]
        end = cumx[rows - 1 : rows]
        x = x_ref[:, cols]
        dtx = dtx_ref[:, cols]
        dy = dy_ref[:, cols]
        weighted = x * dtx
        from_state = jnp.exp(end - cumx) * mul(b_all, split(block_diagonal(later)))
        dxd = dxd_ref[:, cols] + from_state
        skip = skip_ref[0:1, cols]
        dx = dtx * dxd + skip * dy
        spread = ((iota((heads, size), 1) + cols.start) // HEAD_DIM == iota((heads, size), 0)).astype(F32)
        cum_grad = cum_grad + exact(dy * (y_ref[:, cols] - skip * x) - weighted * dxd, spread, MT)
        step_grad = step_grad + exact(x * dxd, spread, MT)
        end_cols = jnp.sum(weighted * from_state, axis=0, keepdims=True) + jnp.exp(end) * jnp.sum(
            later * pair(enter_ref, cols), axis=0, keepdims=True
        )
        ends = ends + exact(jnp.broadcast_to(end_cols, (8, size)), spread, MT)
        skip_cols = jnp.sum(dy * x, axis=0, keepdims=True)
        skips = skips + exact(jnp.broadcast_to(skip_cols, (8, size)), spread, MT)
        dpre = dx * silu_slope(prex_ref[:, cols])
        dxd_ref[:, cols] = dpre
        for k in range(CONV):
            tap = jnp.sum(dpre * extx[HALO - 3 + k : HALO - 3 + k + rows, cols], axis=0, keepdims=True)
            for i in range(2):
                own_p[cols.start // LANES + i, k : k + 1, :] = tap[:, i * LANES : (i + 1) * LANES]
    send_x = remote(dxd_ref.at[0:8, :], next_x, halo_send.at[2], halo_recv.at[2], behind, tp)

    @pl.when(me > 0)
    def _():
        send_x.start()

    triu = (iota((rows, rows), 0) <= iota((rows, rows), 1)).astype(F32)
    log_grad = exact(triu, cum_grad) + ends[0:1]
    raw_grad = (step_grad - rate * log_grad) * sigmoid(jnp.transpose(dtt_ref[...]) + bias_ref[...])
    ddt_ref[...] = jnp.transpose(raw_grad)
    store(ddt_ref, ddt_hbm)
    small = [
        jnp.sum(raw_grad, axis=0, keepdims=True),
        jnp.sum(-rate * log_grad * step, axis=0, keepdims=True),
        skips[0:1],
    ]
    for i in range(3):
        own_p[i, 5:6, 0:heads] = small[i]

    gather_tiles(own_p, slots_p, 6)
    tp_wait(slots_e, 1)
    tp_wait(slots_l, 2)
    slots_e[tp] = early[tp]
    slots_l[tp] = late[tp]
    both = slots_e[0]
    db = slots_l[0]
    for q in range(1, ranks):
        both = both + slots_e[q]
        db = db + slots_l[q]
    for i, grad in ((0, both[0:rows] + db), (1, both[rows:])):
        mine = pl.ds(pl.multiple_of(i * half + tp * LANES, LANES), LANES)
        dpre = grad * silu_slope(prebc_ref[:, mine])
        dpre_own[i, 0:rows, :] = dpre
        for k in range(CONV):
            taps_slots[me, i * CONV + k : i * CONV + k + 1, :] = jnp.sum(
                dpre * extbc[HALO - 3 + k : HALO - 3 + k + rows, mine], axis=0, keepdims=True
            )
    send_bc = remote(dpre_own.at[:, 0:8, :], next_bc, halo_send.at[3], halo_recv.at[3], behind, tp)

    @pl.when(me > 0)
    def _():
        send_bc.start()

    def to_all(i):
        return remote(taps_slots.at[me], taps_slots.at[me], ctx_send.at[8, i], ctx_recv.at[8, me], i, tp)

    for d in range(1, count):
        to_all(lax.rem(me + d, count)).start()

    extx[0:rows, :] = dxd_ref[...]

    @pl.when(me < count - 1)
    def _():
        send_x.wait_recv()
        extx[rows : rows + 8, :] = next_x[...]

    @pl.when(me == count - 1)
    def _():
        extx[rows : rows + 8, :] = jnp.zeros((8, width), F32)

    for cols in tiles(width, LANES):
        total = cx_ref[0:1, cols] * extx[3 : 3 + rows, cols]
        for k in range(1, CONV):
            total = total + cx_ref[k : k + 1, cols] * extx[3 - k : 3 - k + rows, cols]
        gx_ref[:, cols] = total.astype(BF16)
    store(gx_ref, gx_hbm)

    def sum_parts():
        slots_p[me] = own_p[my_part]
        for j in range(count):
            slot_wait(slots_p, 6, j)
        total = slots_p[0]
        for j in range(1, count):
            total = total + slots_p[j]
        outs_p[0] = total
        for d in range(1, count):
            from_owner(outs_p.at[0], total_p, 6, lax.rem(me + d, count)).start()
        total_p[my_part] = total

    owner_only(sum_parts)

    @pl.when(me < count - 1)
    def _():
        send_bc.wait_recv()
        dpre_own[:, rows : rows + 8, :] = next_bc[...]

    @pl.when(me == count - 1)
    def _():
        dpre_own[:, rows : rows + 8, :] = jnp.zeros((2, 8, LANES), F32)

    for i in range(2):
        taps = cbc_ref[:, pl.ds(pl.multiple_of(i * half + tp * LANES, LANES), LANES)]
        total = taps[0:1] * dpre_own[i, 3 : 3 + rows, :]
        for k in range(1, CONV):
            total = total + taps[k : k + 1] * dpre_own[i, 3 - k : 3 - k + rows, :]
        final[tp, i * rows : (i + 1) * rows, :] = total.astype(BF16)
    tp_start(lambda q: final.at[tp], final.at[tp], 3)

    for j in range(count):
        slot_wait(taps_slots, 8, j)
    taps_sum = taps_slots[0]
    for j in range(1, count):
        taps_sum = taps_sum + taps_slots[j]
    taps_all[tp] = taps_sum
    tp_start(lambda q: taps_all.at[tp], taps_all.at[tp], 4)

    settle_exchange(own_p, slots_p, outs_p, total_p, 6)
    for r, cols in enumerate(tiles(width, LANES)):
        small_ref[:, cols] = total_p[r, 0:CONV, :]
        gain_sum[:, cols] = total_p[r, 4:5, :]
    bias_sum[...] = total_p[0, 5:6, 0:heads]
    alog_sum[...] = total_p[1, 5:6, 0:heads]
    skip_sum[...] = total_p[2, 5:6, 0:heads]
    store(small_ref, convx_hbm)
    store(gain_sum, gain_out)
    store(bias_sum, bias_out)
    store(alog_sum, alog_out)
    store(skip_sum, skip_out)

    tp_wait(final, 3)
    for q in range(ranks):
        for i in range(2):
            gbc_ref[i, :, q * STATE : (q + 1) * STATE] = final[q, i * rows : (i + 1) * rows, :]
    store(gbc_ref.at[0], gb_hbm)
    store(gbc_ref.at[1], gc_hbm)
    tp_wait(taps_all, 4)
    for q in range(ranks):
        for i in range(2):
            convbc_ref[i, :, q * STATE : (q + 1) * STATE] = taps_all[q, i * CONV : (i + 1) * CONV, :]
    store(convbc_ref.at[0], convb_hbm)
    store(convbc_ref.at[1], convc_hbm)

    @pl.when(me < count - 1)
    def _():
        for copy in tail:
            copy.wait_send()

    @pl.when(me > 0)
    def _():
        send_x.wait_send()
        send_bc.wait_send()

    drain_f()
    drain_b()
    drain(own_p, slots_p, outs_p, total_p, 6)
    for d in range(1, count):
        to_all(lax.rem(me + d, count)).wait_send()
    for copy in started:
        copy.wait_send()
    for copy in stores:
        copy.wait()


def deliver_kernel(number, *refs):
    held = refs[2 * number : 3 * number]
    arrive, leave = refs[3 * number :]
    incoming = [pltpu.make_async_copy(refs[i], held[i], arrive.at[i]) for i in range(number)]
    outgoing = [pltpu.make_async_copy(held[i], refs[number + i], leave.at[i]) for i in range(number)]
    for copy in incoming:
        copy.start()
    for arrived, copy in zip(incoming, outgoing):
        arrived.wait()
        copy.start()
    for copy in outgoing:
        copy.wait()


def body(
    x_raw, b_raw, c_raw, z_gate, dt_raw, conv_x, conv_b, conv_c, dt_bias, a_log, d_skip, gain, grad_out
):
    rows, width = x_raw.shape
    heads = dt_raw.shape[1]
    half = b_raw.shape[1]
    count, ranks = lax.axis_size("ctx"), lax.axis_size("tp")
    parts = width // LANES
    hbm = pl.BlockSpec(memory_space=pl.ANY)

    def f32(*shape):
        return pltpu.VMEM(shape, F32)

    def b16(*shape):
        return pltpu.VMEM(shape, BF16)

    full, shared = f32(rows, width), f32(rows, 2 * half)
    outs = [
        ((rows, width), BF16), ((rows, half), BF16), ((rows, half), BF16), ((rows, width), BF16), ((heads, rows), F32),
        ((CONV, width), F32), ((CONV, half), F32), ((CONV, half), F32), ((1, heads), F32), ((1, heads), F32),
        ((1, heads), F32), ((1, width), F32),
    ]
    scratch = [
        b16(rows, width), b16(rows, 2 * half), b16(rows, width), f32(heads, rows), f32(CONV, width),
        f32(CONV, 2 * half), f32(1, heads), f32(1, heads), f32(1, heads), f32(1, width), b16(rows, width),
        b16(HALO, width + 2 * half), f32(HALO + rows, width), f32(HALO + rows, 2 * half), full, full, shared, shared,
        f32(heads, rows), full, full, f32(8, width),
        full, full, full, f32(GROUPS, rows, rows), f32(GROUPS, rows, rows),
        f32(parts, ROW_F, LANES), f32(parts // 2, ROW_F, LANES), *[f32(parts // 2, STATE, LANES)] * 3,
        f32(parts, STATE, LANES),
        f32(parts, STATE, LANES), *[f32(parts // 2, STATE, LANES)] * 4, f32(parts, STATE, LANES),
        f32(parts, 8, LANES), f32(count, 8, LANES), f32(1, 8, LANES), f32(parts, 8, LANES), f32(count, 8, LANES),
        f32(ranks, 8, rows), f32(ranks, 2 * rows, LANES), f32(ranks, 2 * rows, LANES), f32(ranks, rows, LANES),
        f32(ranks, rows, LANES), b16(ranks, 2 * rows, LANES), f32(ranks, 8, LANES), f32(2, rows + 8, LANES),
        f32(8, width), f32(2, 8, LANES),
        b16(rows, width), b16(2, rows, half), b16(rows, width), f32(heads, rows), f32(2, CONV, half), f32(CONV, width),
        f32(1, heads), f32(1, heads), f32(1, heads), f32(1, width),
    ] + [
        pltpu.SemaphoreType.DMA(s)
        for s in ((13,), (12,), (9, count), (9, count), (5, ranks), (5, ranks), (4,), (4,))
    ]
    shapes = [jax.ShapeDtypeStruct(s, d) for s, d in outs]
    results = pl.pallas_call(
        mixer_kernel,
        out_shape=shapes,
        in_specs=[hbm] * 13,
        out_specs=[hbm] * len(outs),
        scratch_shapes=scratch,
        compiler_params=pltpu.CompilerParams(
            collective_id=0, has_side_effects=True, vmem_limit_bytes=56 * 1024 * 1024
        ),
    )(
        x_raw, b_raw, c_raw, z_gate, dt_raw.T, conv_x, conv_b, conv_c, dt_bias[None], a_log[None], d_skip[None],
        gain[None], grad_out,
    )
    gx, gb, gc, dz, ddt, convx, convb, convc, bias, alog, skip, gain_grad = pl.pallas_call(
        functools.partial(deliver_kernel, len(outs)),
        out_shape=shapes,
        in_specs=[hbm] * len(outs),
        out_specs=[hbm] * len(outs),
        scratch_shapes=[pltpu.VMEM(s, d) for s, d in outs] + [pltpu.SemaphoreType.DMA((len(outs),))] * 2,
        compiler_params=pltpu.CompilerParams(vmem_limit_bytes=56 * 1024 * 1024),
    )(*results)
    return gx, gb, gc, dz, ddt.T, convx, convb, convc, bias[0], alog[0], skip[0], gain_grad[0]


def solution(mesh):
    col, row, cut = P("ctx", "tp"), P("ctx", None), P("tp")
    return jax.shard_map(
        body,
        mesh=mesh,
        in_specs=(col, row, row, col, col, P(None, "tp"), P(), P(), cut, cut, cut, cut, col),
        out_specs=(col, row, row, col, col, P(None, "tp"), P(), P(), cut, cut, cut, cut),
        check_vma=False,
    )
```
